256 devices in a mesh: src: 32 (over z, x), tgt: 8 (over y, core).
Axes of the slice: x: 4, y: 4, z: 8, core: 2. Of those that a mesh axis runs over, the one named last changes fastest.
Arguments:
- sources: float32 [50, 16384], P(None, 'src'), may hold values from -1.2 to 1.2
- targets: float32 [50, 32768], P(None, 'tgt'), may hold values from -1.2 to 1.2
- pair_active: int32 [32, 8], P('src', 'tgt'), may hold values from 0 to 1, as said below
- count_src: int32 [32], replicated, may hold values from 256 to 512, as said below
- count_tgt: int32 [8], replicated, may hold values from 2048 to 4096, as said below
Outputs:
- source_potential: float32 [16384], P('src')
- target_potential: float32 [32768], P('tgt')
- ancestors: float32 [50, 32768], P(None, ('tgt', 'src'))
The draws below stay inside these ranges and needn't reach their ends.
Inputs may be any that keep to these rules, and one draw needn't show every extreme that they name: `pair_active`: every source block has at least one listed tile and every target tile is listed with at least one source block. `count_src`: some block holds exactly 512 live cells and another exactly 256. `count_tgt`: some tile holds exactly 4096 live cells and another exactly 2048.
All inputs are finite; a program needn't handle non-finite values.
Results may differ from the reference program's by a relative error of at most 0.0003.
Values sent between devices are 32-bit elements; how exact they have to be, the bound alone decides.
A program may use at most 64 MiB of HBM per device.

```python
import jax
import jax.numpy as jnp
from jax import lax

DIMS = 50
SRC_DEV = 512
TILE = 4096
ITERS = 4
SOURCES = 16384
TARGETS = 32768
N_SRC = 32


def counts_with_ends(key, length, most):
    key_one, key_two, key_three = jax.random.split(key, 3)
    values = jax.random.randint(key_one, (length,), most // 2, most + 1)
    first = jax.random.randint(key_two, (), 0, length)
    second = (first + 1 + jax.random.randint(key_three, (), 0, length - 1)) % length
    values = values.at[first].set(most)
    return values.at[second].set(most // 2).astype(jnp.int32)


def draw_pair_active(key, part):
    key = jax.random.fold_in(key, 11)
    tiles = TARGETS // TILE
    listed = jax.random.randint(key, (N_SRC, tiles), 0, 3) > 0
    rows = jnp.arange(N_SRC, dtype=jnp.int32)[:, None]
    cols = jnp.arange(tiles, dtype=jnp.int32)[None, :]
    return (listed | (rows % tiles == cols)).astype(jnp.int32)


def draw_count_src(key, part):
    key = jax.random.fold_in(key, 23)
    return counts_with_ends(key, N_SRC, SRC_DEV)


def draw_count_tgt(key, part):
    key = jax.random.fold_in(key, 37)
    return counts_with_ends(key, TARGETS // TILE, TILE)


def levels(rng, shape, cuts, low, top_value):
    def one(position, parts):
        heights = jax.random.uniform(jax.random.fold_in(jax.random.fold_in(rng, 6), position), (parts,), jnp.float32, low / len(cuts), top_value / len(cuts))
        return jnp.repeat(jnp.exp(heights), shape[position] // parts).reshape((-1,) + (1,) * (len(shape) - position - 1))

    level = one(*cuts[0])
    for cut in cuts[1:]:
        level = level * one(*cut)
    return level


def noise(own_key, dims, width, reach, cuts=(), kind=jnp.bfloat16):
    values = width * jax.random.normal(own_key, dims, jnp.float32)
    if cuts:
        values = values * levels(own_key, dims, cuts, -0.22, 0.18)
    return jnp.clip(values, -reach, reach).astype(kind)


def setup_inputs(seed: int = 0) -> dict:
    streams_of = jax.random.split(jax.random.key(seed), 6)
    return {
        "sources": noise(streams_of[0], (DIMS, SOURCES), 0.2, 1.2, ((1, 32),), jnp.float32),
        "targets": noise(streams_of[1], (DIMS, TARGETS), 0.2, 1.2, ((1, 8),), jnp.float32),
        "pair_active": draw_pair_active(jax.random.fold_in(streams_of[5], 71), 0),
        "count_src": draw_count_src(jax.random.fold_in(streams_of[5], 71), 0),
        "count_tgt": draw_count_tgt(jax.random.fold_in(streams_of[5], 71), 0),
    }


EPS = 0.02
NEG = -1e30


def tile_cost(block, points):
    left = jnp.sum(block * block, axis=0)
    right = jnp.sum(points * points, axis=0)
    cross = lax.dot_general(block, points, (((0,), (0,)), ((), ())), precision=lax.Precision.HIGHEST)
    return left[:, None] + right[None, :] - 2.0 * cross


def reference(sources, targets, pair_active, count_src, count_tgt):
    log_a = -jnp.log(jnp.sum(count_src).astype(jnp.float32))
    log_b = -jnp.log(jnp.sum(count_tgt).astype(jnp.float32))
    within = jnp.arange(TARGETS, dtype=jnp.int32) % TILE
    col_ok = within < jnp.repeat(count_tgt, TILE)
    blocks = sources.reshape(DIMS, N_SRC, SRC_DEV).transpose(1, 0, 2)
    row_all = jnp.arange(SRC_DEV, dtype=jnp.int32)[None, :] < count_src[:, None]
    active_cols = jnp.repeat(pair_active > 0, TILE, axis=1) & col_ok[None, :]
    order = jnp.arange(N_SRC, dtype=jnp.int32)

    def pieces(b):
        cost = tile_cost(blocks[b], targets)
        allowed = row_all[b][:, None] & active_cols[b][None, :]
        return cost, allowed

    def row_step(g):
        def one(b):
            cost, allowed = pieces(b)
            logits = jnp.where(allowed, (g[None, :] - cost) / EPS, NEG)
            peak = jnp.max(logits, axis=1)
            total = jnp.sum(jnp.where(allowed, jnp.exp(logits - peak[:, None]), 0.0), axis=1)
            live = row_all[b]
            return jnp.where(live, EPS * (log_a - peak - jnp.log(jnp.where(live, total, 1.0))), 0.0)
        return lax.map(one, order)

    def column_step(f):
        def one(carry, b):
            cost, allowed = pieces(b)
            logits = jnp.where(allowed, (f[b][:, None] - cost) / EPS, NEG)
            peak = jnp.max(logits, axis=0)
            total = jnp.sum(jnp.where(allowed, jnp.exp(logits - peak[None, :]), 0.0), axis=0)
            best = jnp.maximum(carry[0], peak)
            joined = carry[1] * jnp.exp(carry[0] - best) + total * jnp.exp(peak - best)
            return (best, joined), None
        start = (jnp.full((TARGETS,), NEG, jnp.float32), jnp.zeros((TARGETS,), jnp.float32))
        (peak, total), _ = lax.scan(one, start, order)
        return jnp.where(col_ok, EPS * (log_b - peak - jnp.log(jnp.where(col_ok, total, 1.0))), 0.0)

    g = jnp.zeros((TARGETS,), jnp.float32)
    f = jnp.zeros((N_SRC, SRC_DEV), jnp.float32)
    for step in range(ITERS):
        f = row_step(g)
        g = column_step(f)

    def gather_one(acc, b):
        cost, allowed = pieces(b)
        expo = jnp.where(allowed, (f[b][:, None] + g[None, :] - cost) / EPS - log_b, NEG)
        weight = jnp.where(allowed, jnp.exp(expo), 0.0)
        return acc + jnp.dot(blocks[b], weight, precision=lax.Precision.HIGHEST), None

    ancestors, _ = lax.scan(gather_one, jnp.zeros((DIMS, TARGETS), jnp.float32), order)
    return f.reshape(SOURCES), g, ancestors
```

```python
import functools
import math

import jax
import jax.numpy as jnp
from jax import lax
from jax.experimental import pallas as pl
from jax.experimental.pallas import tpu as pltpu
from jax.sharding import PartitionSpec as P

ITERS = 4
EPS = 0.02
SCALE = math.log2(math.e) / EPS
NEG = -(2.0**100)
LOW = -3.0e38
MESH = pl.DeviceIdType.MESH

DIMS = 50
PAD = 64
ROWS = 1024
COLS = 2048
LANES = 128
ROW_BLOCKS = ROWS // LANES
COL_BLOCKS = COLS // LANES
X_CHIPS = 4
Y_CHIPS = 4
Z_CHIPS = 8
CORES = 2

OVER_XY = sorted(
    [(0, dx, dy, 0) for dx in range(X_CHIPS) for dy in range(Y_CHIPS) if dx or dy],
    key=lambda d: -(min(d[1], X_CHIPS - d[1]) + min(d[2], Y_CHIPS - d[2])),
)
OVER_Z_CORE = sorted(
    [(dz, 0, 0, dc) for dz in range(Z_CHIPS) for dc in range(CORES) if dz or dc],
    key=lambda d: -min(d[0], Z_CHIPS - d[0]),
)
OVER_X_CORE = [(0, dx, 0, dc) for dx in range(X_CHIPS) for dc in range(CORES) if dx or dc]
OVER_X = [(0, 2, 0, 0), (0, 1, 0, 0), (0, 3, 0, 0)]
OTHER_CORE = (0, 0, 0, 1)
PARTNERS = OVER_XY + OVER_Z_CORE + [d for d in OVER_X_CORE if d[1] and d[3]]


def tree(op, parts):
    while len(parts) > 1:
        parts = [op(*parts[i : i + 2]) if i + 1 < len(parts) else parts[i] for i in range(0, len(parts), 2)]
    return parts[0]


def log_sum(parts):
    peak = tree(jnp.maximum, parts)
    total = tree(jnp.add, [jnp.exp2(p - peak) for p in parts])
    return peak + jnp.log2(total)


def split(value, pieces):
    out = []
    for _ in range(pieces):
        piece = value.astype(jnp.bfloat16)
        out.append(piece)
        value = value - piece.astype(jnp.float32)
    return out


def kernel(
    count_src, count_tgt, pair, src, tgt,
    f_out, g_out, anc_out,
    flags, x_in, y_in, x_full, y_full, x_stack, x_lines, y_stack, x_pieces,
    logits, row_peak, row_total, f_rep, g_rep, col_peak, col_total,
    row_box, col_box, f_box, g_box, num_box,
    flag_sems, x_send, x_recv, y_sems, row_send, row_recv, col_send, col_recv, f_sems, g_sems, num_sems,
):
    at_src = lax.axis_index("src")
    at_tgt = lax.axis_index("tgt")
    z, x = at_src // X_CHIPS, lax.rem(at_src, X_CHIPS)
    y, c = at_tgt // CORES, lax.rem(at_tgt, CORES)
    half = x // 2

    def device(d):
        dz, dx, dy, dc = d
        return (
            lax.rem(z + dz, Z_CHIPS) * X_CHIPS + lax.rem(x + dx, X_CHIPS),
            lax.rem(y + dy, Y_CHIPS) * CORES + lax.rem(c + dc, CORES),
        )

    def remote(a, b, send, recv, d):
        return pltpu.make_async_remote_copy(
            src_ref=a, dst_ref=b, send_sem=send, recv_sem=recv, device_id=device(d), device_id_type=MESH
        )

    barrier = pltpu.get_barrier_semaphore()
    for d in PARTNERS:
        pl.semaphore_signal(barrier, inc=1, device_id=device(d), device_id_type=MESH)

    mine = x * CORES + c
    listed = (pair[0, 0] > 0).astype(jnp.float32)
    flags[mine] = jnp.full((1, LANES), listed, jnp.float32)
    for k in range(Z_CHIPS):
        at = pl.multiple_of((k * X_CHIPS + x) * LANES, LANES)
        y_in[c, :, k * LANES : (k + 1) * LANES] = tgt[:, pl.ds(at, LANES)]

    pl.semaphore_wait(barrier, len(PARTNERS))

    y_copy = remote(y_in.at[c], y_in.at[c], y_sems.at[0], y_sems.at[1], OTHER_CORE)
    y_copy.start()
    x_copies = [remote(src, x_in.at[lax.rem(x, 2)], x_send, x_recv.at[lax.rem(x, 2)], d) for d in OVER_X]

    @pl.when(half == c)
    def _():
        for copy in x_copies:
            copy.start()
        x_in[lax.rem(x, 2)] = src[...]

    flag_copies = [remote(flags.at[mine], flags.at[mine], flag_sems.at[0], flag_sems.at[1], d) for d in OVER_X_CORE]
    for copy in flag_copies:
        copy.start()

    def number_of(counts, length):
        total = counts[0]
        for i in range(1, length):
            total = total + counts[i]
        return total.astype(jnp.float32)

    log_a = -jnp.log2(jnp.full((8, LANES), number_of(count_src, Z_CHIPS * X_CHIPS), jnp.float32))
    log_b = -jnp.log2(jnp.full((COL_BLOCKS, LANES), number_of(count_tgt, Y_CHIPS * CORES), jnp.float32))
    row_counts = [count_src[z * X_CHIPS + 2 * c + i] for i in range(2)]
    col_counts = [count_tgt[y * CORES + i] for i in range(CORES)]

    def row_ok(block, lane):
        within = lax.rem(block, 4) * LANES + lane
        return within < jnp.where(block < 4, row_counts[0], row_counts[1])

    def col_ok(block, lane):
        within = (lax.rem(block, Z_CHIPS) * X_CHIPS + x) * LANES + lane
        return within < jnp.where(block < Z_CHIPS, col_counts[0], col_counts[1])

    def places(shape):
        return lax.broadcasted_iota(jnp.int32, shape, 0), lax.broadcasted_iota(jnp.int32, shape, 1)

    row_live = row_ok(*places((ROW_BLOCKS, LANES)))
    col_live = col_ok(*places((COL_BLOCKS, LANES)))
    along_rows = lax.broadcasted_iota(jnp.int32, (1, ROWS), 1)
    along_cols = lax.broadcasted_iota(jnp.int32, (1, COLS), 1)
    dead_rows = jnp.where(row_ok(along_rows // LANES, lax.rem(along_rows, LANES)), 0.0, NEG)
    dead_cols = jnp.where(col_ok(along_cols // LANES, lax.rem(along_cols, LANES)), 0.0, NEG)

    def flags_received():
        d = remote(flags.at[pl.ds(0, len(OVER_X_CORE))], flags.at[pl.ds(0, len(OVER_X_CORE))], flag_sems.at[0], flag_sems.at[1], OTHER_CORE)
        d.wait_recv()
        d.wait_send()

    flags_received()

    @pl.when(x != 2 * c)
    def _():
        remote(x_in.at[0], x_in.at[0], x_send, x_recv.at[0], OVER_X[0]).wait_recv()

    @pl.when(x != 2 * c + 1)
    def _():
        remote(x_in.at[1], x_in.at[1], x_send, x_recv.at[1], OVER_X[0]).wait_recv()

    x_full[DIMS:PAD, :] = jnp.zeros((PAD - DIMS, ROWS), jnp.float32)
    for i in range(2):
        x_full[0:DIMS, i * 512 : (i + 1) * 512] = x_in[i]
    first, second = split(x_full[...], 2)
    x_pieces[0:PAD, :] = first
    x_pieces[PAD:, :] = second
    x_full[0:DIMS, :] = x_full[0:DIMS, :] * (2.0 * SCALE)
    x_full[DIMS : DIMS + 1, :] = jnp.where(along_rows < 512, 1.0, 0.0)
    x_full[DIMS + 1 : DIMS + 2, :] = jnp.where(along_rows < 512, 0.0, 1.0)
    x_full[DIMS + 2 : DIMS + 3, :] = dead_rows
    p1, p2, p3 = split(x_full[...], 3)
    for i, p in enumerate((p1, p1, p2, p1, p3, p2)):
        x_stack[i * PAD : (i + 1) * PAD, :] = p
    for i in range(ROW_BLOCKS):
        x_lines[i * LANES : (i + 1) * LANES, :] = x_stack[:, i * LANES : (i + 1) * LANES].T

    y_copy.wait_recv()
    y_full[DIMS:PAD, :] = jnp.zeros((PAD - DIMS, COLS), jnp.float32)
    for i in range(CORES):
        at = pl.ds(i * (COLS // 2), COLS // 2)
        y_full[0:DIMS, at] = y_in[i]
        for k in range(2):
            unlisted = jnp.where(flags[(2 * c + k) * CORES + i] > 0, 0.0, NEG)
            y_full[DIMS + k : DIMS + k + 1, at] = jnp.concatenate([unlisted] * Z_CHIPS, axis=1)
    y_full[DIMS : DIMS + 1, :] = jnp.minimum(y_full[DIMS : DIMS + 1, :], dead_cols)
    y_full[DIMS + 1 : DIMS + 2, :] = jnp.minimum(y_full[DIMS + 1 : DIMS + 2, :], dead_cols)
    y_full[DIMS + 2 : DIMS + 3, :] = jnp.ones((1, COLS), jnp.float32)
    for b in range(COL_BLOCKS):
        block = y_full[0:DIMS, b * LANES : (b + 1) * LANES]
        first_g = -SCALE * jnp.sum(block * block, axis=0, keepdims=True)
        g_rep[b] = jnp.broadcast_to(first_g, (8, LANES))
        p1, p2, p3 = split(y_full[:, b * LANES : (b + 1) * LANES], 3)
        for i, p in enumerate((p1, p2, p1, p3, p1, p2)):
            y_stack[i * PAD : (i + 1) * PAD, b * LANES : (b + 1) * LANES] = p

    def logits_of(k, _):
        at = pl.ds(pl.multiple_of(k * 256, 256), 256)
        logits[:, at] = jnp.dot(x_lines[...], y_stack[:, at], preferred_element_type=jnp.float32)
        return 0

    lax.fori_loop(0, COLS // 256, logits_of, 0)

    def row_step(it):
        g = [g_rep[b] for b in range(COL_BLOCKS)]

        def body(k, _):
            at = pl.ds(pl.multiple_of(k * 8, 8), 8)
            parts = [logits[at, b * LANES : (b + 1) * LANES] + g[b] for b in range(COL_BLOCKS)]
            peak = tree(jnp.maximum, parts)
            row_peak[at, :] = peak
            row_total[at, :] = tree(jnp.add, [jnp.exp2(p - peak) for p in parts])
            return 0

        lax.fori_loop(0, ROWS // 8, body, 0, unroll=4)
        own = row_box.at[it, len(OVER_XY)]
        for b in range(ROW_BLOCKS):
            peaks = row_peak[b * LANES : (b + 1) * LANES, :].T
            totals = row_total[b * LANES : (b + 1) * LANES, :].T
            peak = jnp.max(peaks, axis=0, keepdims=True)
            total = jnp.sum(totals * jnp.exp2(peaks - peak), axis=0, keepdims=True)
            own[b : b + 1, :] = peak + jnp.log2(total)
        for r, d in enumerate(OVER_XY):
            remote(own, row_box.at[it, r], row_send.at[it], row_recv.at[it], d).start()
        row_all(it).wait_recv()
        total = log_sum([row_box[it, r] for r in range(len(OVER_XY) + 1)])
        f = jnp.where(row_live, log_a - total, 0.0)
        for b in range(ROW_BLOCKS):
            f_rep[b * LANES : (b + 1) * LANES, :] = jnp.broadcast_to(f[b : b + 1, :], (LANES, LANES)).T
        return f

    def row_all(it):
        some = row_box.at[it, pl.ds(0, len(OVER_XY))]
        return remote(some, some, row_send.at[it], row_recv.at[it], OVER_XY[0])

    def col_start(it):
        def pair_of_blocks(q, _):
            cols = [pl.ds(pl.multiple_of((2 * q + i) * LANES, LANES), LANES) for i in range(2)]

            def body(k, carry):
                base = pl.multiple_of(k * 64, 64)
                f = [f_rep[pl.ds(base + 8 * j, 8), :] for j in range(8)]
                out = []
                for i in range(2):
                    peak, total = carry[2 * i : 2 * i + 2]
                    parts = [logits[pl.ds(base + 8 * j, 8), cols[i]] + f[j] for j in range(8)]
                    best = jnp.maximum(peak, tree(jnp.maximum, parts))
                    fresh = tree(jnp.add, [jnp.exp2(p - best) for p in parts])
                    out += [best, total * jnp.exp2(peak - best) + fresh]
                return tuple(out)

            low, zero = jnp.full((8, LANES), LOW, jnp.float32), jnp.zeros((8, LANES), jnp.float32)
            done = lax.fori_loop(0, ROWS // 64, body, (low, zero, low, zero), unroll=4)
            for i in range(2):
                col_peak[2 * q + i] = done[2 * i]
                col_total[2 * q + i] = done[2 * i + 1]
            return 0

        lax.fori_loop(0, COL_BLOCKS // 2, pair_of_blocks, 0)
        own = col_box.at[it, len(OVER_Z_CORE)]
        peaks = col_peak[...]
        peak = jnp.max(peaks, axis=1, keepdims=True)
        total = jnp.sum(col_total[...] * jnp.exp2(peaks - peak), axis=1)
        own[...] = peak[:, 0, :] + jnp.log2(total)
        for r, d in enumerate(OVER_Z_CORE):
            remote(own, col_box.at[it, r], col_send.at[it], col_recv.at[it], d).start()

    def col_all(it):
        some = col_box.at[it, pl.ds(0, len(OVER_Z_CORE))]
        return remote(some, some, col_send.at[it], col_recv.at[it], OVER_Z_CORE[0])

    def col_end(it):
        col_all(it).wait_recv()
        total = log_sum([col_box[it, r] for r in range(len(OVER_Z_CORE) + 1)])
        return jnp.where(col_live, log_b - total, 0.0)

    def iteration(it, _):
        row_step(it)
        col_start(it)
        g = col_end(it)
        for b in range(COL_BLOCKS):
            g_rep[b] = jnp.broadcast_to(g[b : b + 1, :], (8, LANES))
        return 0

    lax.fori_loop(0, ITERS - 1, iteration, 0)
    last = ITERS - 1
    f_box[0] = row_step(last)
    f_copy = remote(f_box.at[0], f_box.at[1], f_sems.at[0], f_sems.at[1], OTHER_CORE)
    f_copy.start()
    col_start(last)

    for b in range(COL_BLOCKS):
        col_peak[b] = jnp.broadcast_to(col_box[last, len(OVER_Z_CORE), b : b + 1, :], (8, LANES))

    def ancestors_of(k, _):
        step = (k + 1) // 2
        dz = jnp.where(lax.rem(k, 2) == 0, 4 + step, 4 - step)
        to = lax.rem(z + dz, Z_CHIPS)
        cols = [pl.ds(pl.multiple_of((i * Z_CHIPS + to) * LANES, LANES), LANES) for i in range(CORES)]
        local = [col_peak[i * Z_CHIPS + to] for i in range(CORES)]
        acc = jnp.zeros((PAD, CORES * LANES), jnp.float32)
        for r in range(ROWS // 256):
            at = slice(r * 256, (r + 1) * 256)
            f = f_rep[at, :]
            weight = jnp.concatenate(
                [jnp.exp2(logits[at, cols[i]] + (f - local[i][0:1, :])) for i in range(CORES)], axis=1
            )
            w1, w2 = split(weight, 2)
            both = jnp.dot(x_pieces[:, at], w1, preferred_element_type=jnp.float32)
            acc += both[0:PAD] + both[PAD:] + jnp.dot(x_pieces[0:PAD, at], w2, preferred_element_type=jnp.float32)
        for i in range(CORES):
            dc = lax.rem(i + c, CORES)
            slot = dc * Z_CHIPS + dz
            num_box[0, slot] = acc[0:56, i * LANES : (i + 1) * LANES]
            num_box[0, slot, DIMS : DIMS + 1, :] = local[i][0:1, :]

            @pl.when(slot != 0)
            def _():
                remote(num_box.at[0, slot], num_box.at[1, slot], num_sems.at[0], num_sems.at[1], (dz, 0, 0, dc)).start()

        return 0

    lax.fori_loop(0, Z_CHIPS, ancestors_of, 0)

    g = col_end(last)
    g_box[x] = jnp.where(c == 0, g[0:Z_CHIPS], g[Z_CHIPS:])
    g_copies = [remote(g_box.at[x], g_box.at[x], g_sems.at[0], g_sems.at[1], d) for d in OVER_X]
    for copy in g_copies:
        copy.start()

    f_copy.wait_recv()
    f_here = f_box[jnp.where(half == c, 0, 1)]
    f_here = jnp.where(lax.rem(x, 2) == 0, f_here[0:4], f_here[4:8])
    block = src[...]
    norms = jnp.sum(block * block, axis=0, keepdims=True)
    count_here = count_src[at_src]
    lane = lax.broadcasted_iota(jnp.int32, (1, LANES), 1)
    for b in range(4):
        line = f_here[b : b + 1, :] * (1.0 / SCALE) + norms[:, b * LANES : (b + 1) * LANES]
        f_out[:, b * LANES : (b + 1) * LANES] = jnp.where(b * LANES + lane < count_here, line, 0.0)

    g_some = remote(g_box.at[pl.ds(0, 3)], g_box.at[pl.ds(0, 3)], g_sems.at[0], g_sems.at[1], OVER_X[0])
    g_some.wait_recv()
    g_some.wait_send()
    count_tile = count_tgt[at_tgt]
    for k in range(Z_CHIPS):
        for i in range(X_CHIPS):
            b = k * X_CHIPS + i
            block = tgt[:, b * LANES : (b + 1) * LANES]
            line = g_box[i, k : k + 1, :] * (1.0 / SCALE) + jnp.sum(block * block, axis=0, keepdims=True)
            g_out[:, b * LANES : (b + 1) * LANES] = jnp.where(b * LANES + lane < count_tile, line, 0.0)

    num_all = remote(
        num_box.at[1, pl.ds(1, 15)], num_box.at[1, pl.ds(1, 15)], num_sems.at[0], num_sems.at[1], OTHER_CORE
    )
    num_all.wait_recv()
    parts = [num_box.at[0, 0]] + [num_box.at[1, r] for r in range(1, 16)]
    weigh = [p[DIMS : DIMS + 1, :] for p in parts]
    total = log_sum(weigh)
    acc = jnp.zeros((DIMS, LANES), jnp.float32)
    for p, w in zip(parts, weigh):
        acc += p[0:DIMS, :] * jnp.exp2(w - total)
    anc_out[...] = jnp.where(at_src * LANES + lane < count_tile, acc, 0.0)

    num_all.wait_send()
    f_copy.wait_send()
    y_copy.wait_send()

    @pl.when(half == c)
    def _():
        for copy in x_copies:
            copy.wait_send()

    def sent(it, _):
        row_all(it).wait_send()
        col_all(it).wait_send()
        return 0

    lax.fori_loop(0, ITERS, sent, 0)


def shards(sources, targets, pair_active, count_src, count_tgt):
    f32, bf16 = jnp.float32, jnp.bfloat16
    vmem, sem = pltpu.VMEM, pltpu.SemaphoreType.DMA
    in_vmem = pl.BlockSpec(memory_space=pltpu.VMEM)
    in_smem = pl.BlockSpec(memory_space=pltpu.SMEM)
    f, g, anc = pl.pallas_call(
        kernel,
        out_shape=(
            jax.ShapeDtypeStruct((1, 512), f32),
            jax.ShapeDtypeStruct((1, 4096), f32),
            jax.ShapeDtypeStruct((DIMS, LANES), f32),
        ),
        in_specs=[in_smem, in_smem, in_smem, in_vmem, in_vmem],
        out_specs=(in_vmem, in_vmem, in_vmem),
        scratch_shapes=[
            vmem((X_CHIPS * CORES, 1, LANES), f32),
            vmem((2, DIMS, 512), f32),
            vmem((CORES, DIMS, COLS // 2), f32),
            vmem((PAD, ROWS), f32),
            vmem((PAD, COLS), f32),
            vmem((6 * PAD, ROWS), bf16),
            vmem((ROWS, 6 * PAD), bf16),
            vmem((6 * PAD, COLS), bf16),
            vmem((2 * PAD, ROWS), bf16),
            vmem((ROWS, COLS), f32),
            vmem((ROWS, LANES), f32),
            vmem((ROWS, LANES), f32),
            vmem((ROWS, LANES), f32),
            vmem((COL_BLOCKS, 8, LANES), f32),
            vmem((COL_BLOCKS, 8, LANES), f32),
            vmem((COL_BLOCKS, 8, LANES), f32),
            vmem((ITERS, 16, ROW_BLOCKS, LANES), f32),
            vmem((ITERS, 16, COL_BLOCKS, LANES), f32),
            vmem((2, ROW_BLOCKS, LANES), f32),
            vmem((X_CHIPS, Z_CHIPS, LANES), f32),
            vmem((2, 16, 56, LANES), f32),
            sem((2,)), sem(()), sem((2,)), sem((2,)), sem((ITERS,)), sem((ITERS,)), sem((ITERS,)), sem((ITERS,)),
            sem((2,)), sem((2,)), sem((2,)),
        ],
        compiler_params=pltpu.CompilerParams(
            collective_id=0, has_side_effects=True, vmem_limit_bytes=40 * 2**20
        ),
    )(count_src, count_tgt, pair_active, sources, targets)
    return f.reshape(512), g.reshape(4096), anc


def solution(mesh):
    return jax.shard_map(
        shards,
        mesh=mesh,
        in_specs=(P(None, "src"), P(None, "tgt"), P("src", "tgt"), P(), P()),
        out_specs=(P("src"), P("tgt"), P(None, ("tgt", "src"))),
        check_vma=False,
    )
```

```python
import math

import jax
import jax.numpy as jnp
from jax import lax
from jax.experimental import pallas as pl
from jax.experimental.pallas import tpu as pltpu
from jax.sharding import PartitionSpec as P

ITERS = 4
EPS = 0.02
SCALE = math.log2(math.e) / EPS
NEG = -(2.0**100)
LOW = -3.0e38
MESH = pl.DeviceIdType.MESH

DIMS = 50
PAD = 64
EXTRA = 16
ROWS = 1024
COLS = 2048
LANES = 128
COL_BLOCKS = COLS // LANES
X_CHIPS = 4
Y_CHIPS = 4
Z_CHIPS = 8
CORES = 2

OVER_XY = sorted(
    [(0, dx, dy, 0) for dx in range(X_CHIPS) for dy in range(Y_CHIPS) if dx or dy],
    key=lambda d: -(min(d[1], X_CHIPS - d[1]) + min(d[2], Y_CHIPS - d[2])),
)
OVER_Z_CORE = sorted(
    [(dz, 0, 0, dc) for dz in range(Z_CHIPS) for dc in range(CORES) if dz or dc],
    key=lambda d: -min(d[0], Z_CHIPS - d[0]),
)
OVER_X_CORE = [(0, dx, 0, dc) for dx in range(X_CHIPS) for dc in range(CORES) if dx or dc]
OVER_X = [(0, 2, 0, 0), (0, 1, 0, 0), (0, 3, 0, 0)]
OTHER_CORE = (0, 0, 0, 1)
PARTNERS = OVER_XY + OVER_Z_CORE + [d for d in OVER_X_CORE if d[1] and d[3]]


def tree(op, parts):
    while len(parts) > 1:
        parts = [op(*parts[i : i + 2]) if i + 1 < len(parts) else parts[i] for i in range(0, len(parts), 2)]
    return parts[0]


def log_sum(parts):
    peak = tree(jnp.maximum, parts)
    total = tree(jnp.add, [jnp.exp2(p - peak) for p in parts])
    return peak + jnp.log2(total)


def split(value, pieces):
    out = []
    for _ in range(pieces):
        piece = value.astype(jnp.bfloat16)
        out.append(piece)
        value = value - piece.astype(jnp.float32)
    return out


def kernel(
    count_src, count_tgt, pair, src, tgt,
    f_out, g_out, anc_out,
    x_own, flags, x_in, y_in, x_full, y_full, x_stack, x_lines, y_stack, x_pieces, y_norms,
    logits, row_peak, row_total, f_rep, g_rep, col_peak, col_total,
    row_box, col_box, f_box, g_box, num_own, num_give, num_got, num_send, num_in,
    own_sems, flag_sems, x_send, x_recv, y_sems, row_send, row_recv, col_send, col_recv, pair_sems, f_sems, g_sems,
    give_send, give_recv, num_sems,
):
    at_src = lax.axis_index("src")
    at_tgt = lax.axis_index("tgt")
    z, x = at_src // X_CHIPS, lax.rem(at_src, X_CHIPS)
    y, c = at_tgt // CORES, lax.rem(at_tgt, CORES)
    half = x // 2

    def device(d):
        dz, dx, dy, dc = d
        return (
            lax.rem(z + dz, Z_CHIPS) * X_CHIPS + lax.rem(x + dx, X_CHIPS),
            lax.rem(y + dy, Y_CHIPS) * CORES + lax.rem(c + dc, CORES),
        )

    def remote(a, b, send, recv, d):
        return pltpu.make_async_remote_copy(
            src_ref=a, dst_ref=b, send_sem=send, recv_sem=recv, device_id=device(d), device_id_type=MESH
        )

    def lanes(k, width=LANES):
        return pl.ds(pl.multiple_of(k * width, width), width)

    barrier = pltpu.get_barrier_semaphore()
    for d in PARTNERS:
        pl.semaphore_signal(barrier, inc=1, device_id=device(d), device_id_type=MESH)

    x_local = pltpu.make_async_copy(src, x_own, own_sems.at[0])
    x_local.start()
    y_local = [
        pltpu.make_async_copy(tgt.at[:, lanes(k * X_CHIPS + x)], y_in.at[c, :, lanes(k)], own_sems.at[1 + k])
        for k in range(Z_CHIPS)
    ]
    for copy in y_local:
        copy.start()
    mine = x * CORES + c
    listed = (pair[0, 0] > 0).astype(jnp.float32)
    flags[mine] = jnp.full((1, LANES), listed, jnp.float32)
    x_local.wait()
    for copy in y_local:
        copy.wait()
    pl.semaphore_wait(barrier, len(PARTNERS))

    x_copies = [remote(x_own, x_in.at[lax.rem(x, 2)], x_send, x_recv.at[lax.rem(x, 2)], d) for d in OVER_X]

    @pl.when(half == c)
    def _():
        for copy in x_copies:
            copy.start()

    y_copy = remote(y_in.at[c], y_in.at[c], y_sems.at[0], y_sems.at[1], OTHER_CORE)
    y_copy.start()
    for d in OVER_X_CORE:
        remote(flags.at[mine], flags.at[mine], flag_sems.at[0], flag_sems.at[1], d).start()

    def number_of(counts, length):
        total = counts[0]
        for i in range(1, length):
            total = total + counts[i]
        return total.astype(jnp.float32)

    log_a = -jnp.log2(jnp.full((4, LANES), number_of(count_src, Z_CHIPS * X_CHIPS), jnp.float32))
    log_b = -jnp.log2(jnp.full((COL_BLOCKS, LANES), number_of(count_tgt, Y_CHIPS * CORES), jnp.float32))
    col_counts = [count_tgt[y * CORES + i] for i in range(CORES)]

    def places(shape):
        return lax.broadcasted_iota(jnp.int32, shape, 0), lax.broadcasted_iota(jnp.int32, shape, 1)

    def row_live(h):
        block, lane = places((4, LANES))
        return block * LANES + lane < count_src[z * X_CHIPS + 2 * c + h]

    block, lane = places((COL_BLOCKS, LANES))
    within = (lax.rem(block, Z_CHIPS) * X_CHIPS + x) * LANES + lane
    col_live = within < jnp.where(block < Z_CHIPS, col_counts[0], col_counts[1])

    x_full[DIMS:PAD, :] = jnp.zeros((PAD - DIMS, ROWS), jnp.float32)
    y_full[DIMS:PAD, :] = jnp.zeros((PAD - DIMS, COLS), jnp.float32)

    def columns_of(tile):
        y_full[0:DIMS, lanes(tile, COLS // 2)] = y_in[tile]

        def body(k, _):
            b = tile * Z_CHIPS + k
            whole = y_full[:, lanes(b)]
            norm = jnp.sum(whole * whole, axis=0, keepdims=True)
            y_norms[b] = norm
            g_rep[b] = jnp.broadcast_to(-SCALE * norm, (8, LANES))
            p1, p2, p3 = split(whole, 3)
            for i, p in enumerate((p1, p2, p1, p3, p1, p2)):
                y_stack[i * PAD : (i + 1) * PAD, lanes(b)] = p
            return 0

        lax.fori_loop(0, Z_CHIPS, body, 0)

    columns_of(c)
    y_copy.wait_recv()
    columns_of(1 - c)
    flag_some = flags.at[pl.ds(0, len(OVER_X_CORE))]
    flag_all = remote(flag_some, flag_some, flag_sems.at[0], flag_sems.at[1], OTHER_CORE)
    flag_all.wait_recv()
    line, lane = places((EXTRA, LANES))
    for b in range(COL_BLOCKS):
        tile, k = b // Z_CHIPS, b % Z_CHIPS
        dead = jnp.where((k * X_CHIPS + x) * LANES + lane < col_counts[tile], 0.0, NEG)
        rows = [jnp.minimum(jnp.where(flags[(2 * c + i) * CORES + tile] > 0, 0.0, NEG), dead) for i in range(2)]
        extra = jnp.where(line == 0, rows[0], jnp.where(line == 1, rows[1], jnp.where(line == 2, 1.0, 0.0)))
        y_stack[6 * PAD :, b * LANES : (b + 1) * LANES] = extra.astype(jnp.bfloat16)

    def rows_of(h):
        live = count_src[z * X_CHIPS + 2 * c + h]
        x_full[0:DIMS, lanes(h, 512)] = x_in[h]
        for b in range(4):
            at = lanes(4 * h + b)
            whole = x_full[:, at]
            q1, q2 = split(whole, 2)
            x_pieces[0:PAD, at] = q1
            x_pieces[PAD:, at] = q2
            p1, p2, p3 = split(whole * (2.0 * SCALE), 3)
            for i, p in enumerate((p1, p1, p2, p1, p3, p2)):
                x_stack[i * PAD : (i + 1) * PAD, at] = p
            dead = jnp.where(b * LANES + lane < live, 0.0, NEG)
            extra = jnp.where(line == 2, dead, jnp.where(line == h, 1.0, 0.0))
            x_stack[6 * PAD :, at] = extra.astype(jnp.bfloat16)
            x_lines[at, :] = x_stack[:, at].T

        def logits_of(k, _):
            logits[lanes(h, 512), lanes(k, 256)] = jnp.dot(
                x_lines[lanes(h, 512), :], y_stack[:, lanes(k, 256)], preferred_element_type=jnp.float32
            )
            return 0

        lax.fori_loop(0, COLS // 256, logits_of, 0)

    def row_all(it, h):
        some = row_box.at[it, h, pl.ds(0, len(OVER_XY))]
        return remote(some, some, row_send.at[it, h], row_recv.at[it, h], OVER_XY[0])

    def row_start(it, h):
        def body(k, _):
            base = h * 512 + k * LANES
            for part in range(2):
                g = [g_rep[b] for b in range(part * 8, part * 8 + 8)]
                for q in range(16):
                    at = pl.ds(pl.multiple_of(base + 8 * q, 8), 8)
                    parts = [logits[at, (part * 8 + b) * LANES : (part * 8 + b + 1) * LANES] + g[b] for b in range(8)]
                    best = tree(jnp.maximum, parts)
                    if part:
                        peak = row_peak[at, :]
                        best = jnp.maximum(best, peak)
                    total = tree(jnp.add, [jnp.exp2(p - best) for p in parts])
                    if part:
                        total += row_total[at, :] * jnp.exp2(peak - best)
                    row_peak[at, :] = best
                    row_total[at, :] = total
            return 0

        lax.fori_loop(0, 4, body, 0)
        own = row_box.at[it, h, len(OVER_XY)]
        for b in range(4):
            peaks = row_peak[lanes(4 * h + b), :].T
            totals = row_total[lanes(4 * h + b), :].T
            peak = jnp.max(peaks, axis=0, keepdims=True)
            total = jnp.sum(totals * jnp.exp2(peaks - peak), axis=0, keepdims=True)
            own[b : b + 1, :] = peak + jnp.log2(total)
        for r, d in enumerate(OVER_XY):
            remote(own, row_box.at[it, h, r], row_send.at[it, h], row_recv.at[it, h], d).start()

    def row_end(it, h):
        row_all(it, h).wait_recv()
        total = log_sum([row_box[it, h, r] for r in range(len(OVER_XY) + 1)])
        f = jnp.where(row_live(h), log_a - total, 0.0)
        for b in range(4):
            f_rep[lanes(4 * h + b), :] = jnp.broadcast_to(f[b : b + 1, :], (LANES, LANES)).T
        return f

    def col_sums(h):
        def body(k, _):
            base = h * 512 + k * 64
            f = [f_rep[pl.ds(pl.multiple_of(base + 8 * j, 8), 8), :] for j in range(8)]
            for b in range(COL_BLOCKS):
                parts = [
                    logits[pl.ds(pl.multiple_of(base + 8 * j, 8), 8), b * LANES : (b + 1) * LANES] + f[j]
                    for j in range(8)
                ]
                peak = col_peak[b]
                best = jnp.maximum(peak, tree(jnp.maximum, parts))
                fresh = tree(jnp.add, [jnp.exp2(p - best) for p in parts])
                col_total[b] = col_total[b] * jnp.exp2(peak - best) + fresh
                col_peak[b] = best
            return 0

        lax.fori_loop(0, 8, body, 0, unroll=4)

    def col_reset():
        col_peak[...] = jnp.full((COL_BLOCKS, 8, LANES), LOW, jnp.float32)
        col_total[...] = jnp.zeros((COL_BLOCKS, 8, LANES), jnp.float32)

    def col_start(it):
        own = col_box.at[it, len(OVER_Z_CORE)]
        peaks = col_peak[...]
        peak = jnp.max(peaks, axis=1, keepdims=True)
        total = jnp.sum(col_total[...] * jnp.exp2(peaks - peak), axis=1)
        own[...] = peak[:, 0, :] + jnp.log2(total)
        return own

    def col_all(it, count):
        some = col_box.at[it, pl.ds(0, count)]
        return remote(some, some, col_send.at[it], col_recv.at[it], OVER_Z_CORE[0])

    def col_value(it):
        total = log_sum([col_box[it, r] for r in range(len(OVER_Z_CORE) + 1)])
        return jnp.where(col_live, log_b - total, 0.0)

    for k in range(2):
        h = lax.rem(k + x, 2)

        @pl.when(x == 2 * c + h)
        def _():
            x_in[h] = x_own[...]

        @pl.when(x != 2 * c + h)
        def _():
            remote(x_in.at[h], x_in.at[h], x_send, x_recv.at[h], OVER_X[0]).wait_recv()

        rows_of(h)
        row_start(0, h)

    def iteration(it, _):
        col_reset()
        for h in range(2):
            row_end(it, h)
            col_sums(h)
        own = col_start(it)
        for r, d in enumerate(OVER_Z_CORE):
            remote(own, col_box.at[it, r], col_send.at[it], col_recv.at[it], d).start()
        col_all(it, len(OVER_Z_CORE)).wait_recv()
        g = col_value(it)
        for b in range(COL_BLOCKS):
            g_rep[b] = jnp.broadcast_to(g[b : b + 1, :], (8, LANES))
        for h in range(2):
            row_start(it + 1, h)
        return 0

    last = ITERS - 1
    lax.fori_loop(0, last, iteration, 0)
    col_reset()
    for h in range(2):
        f_box[0, h] = row_end(last, h)
        col_sums(h)
    own = col_start(last)
    other = len(OVER_Z_CORE) - 1
    pair_copy = remote(own, col_box.at[last, other], pair_sems.at[0], pair_sems.at[1], OTHER_CORE)
    pair_copy.start()
    for r, d in enumerate(OVER_Z_CORE[:other]):
        remote(own, col_box.at[last, r], col_send.at[last], col_recv.at[last], d).start()
    f_copy = remote(f_box.at[0], f_box.at[1], f_sems.at[0], f_sems.at[1], OTHER_CORE)
    f_copy.start()
    pair_copy.wait_recv()
    both = log_sum([own[...], col_box[last, other]])
    for b in range(COL_BLOCKS):
        col_peak[b] = jnp.broadcast_to(both[b : b + 1, :], (8, LANES))

    def distance(k):
        step = (k + 1) // 2
        return jnp.where(lax.rem(k, 2) == 0, 4 + step, 4 - step)

    def give(k):
        return remote(num_give.at[k], num_got.at[k], give_send, give_recv.at[k], OTHER_CORE)

    def ancestors_of(k, _):
        @pl.when(k < Z_CHIPS)
        def _():
            to = lax.rem(z + distance(k), Z_CHIPS)
            cols = [lanes(i * Z_CHIPS + to) for i in range(CORES)]
            local = [col_peak[i * Z_CHIPS + to] for i in range(CORES)]
            acc = jnp.zeros((PAD, CORES * LANES), jnp.float32)
            for r in range(ROWS // 256):
                at = slice(r * 256, (r + 1) * 256)
                f = f_rep[at, :]
                weight = jnp.concatenate(
                    [jnp.exp2(logits[at, cols[i]] + (f - local[i][0:1, :])) for i in range(CORES)], axis=1
                )
                w1, w2 = split(weight, 2)
                two = jnp.dot(x_pieces[:, at], w1, preferred_element_type=jnp.float32)
                acc += two[0:PAD] + two[PAD:] + jnp.dot(x_pieces[0:PAD, at], w2, preferred_element_type=jnp.float32)
            tiles = [acc[0:56, i * LANES : (i + 1) * LANES] for i in range(CORES)]
            num_own[k] = jnp.where(c == 0, tiles[0], tiles[1])
            num_give[k] = jnp.where(c == 0, tiles[1], tiles[0])
            give(k).start()

        @pl.when(k >= 2)
        def _():
            j = k - 2
            dz = distance(j)
            give(j).wait_recv()
            num_send[j] = num_own[j] + num_got[j]
            num_send[j, DIMS : DIMS + 1, :] = col_peak[c * Z_CHIPS + lax.rem(z + dz, Z_CHIPS)][0:1, :]

            @pl.when(j < Z_CHIPS - 1)
            def _():
                remote(num_send.at[j], num_in.at[j], num_sems.at[0], num_sems.at[1], (dz, 0, 0, 0)).start()

        return 0

    lax.fori_loop(0, Z_CHIPS + 2, ancestors_of, 0)

    col_all(last, other).wait_recv()
    g = col_value(last)
    g_here = jnp.where(c == 0, g[0:Z_CHIPS], g[Z_CHIPS:]) * (1.0 / SCALE)
    for k in range(Z_CHIPS):
        norm = y_norms[c * Z_CHIPS + k]
        within = (k * X_CHIPS + x) * LANES + lax.broadcasted_iota(jnp.int32, (1, LANES), 1)
        g_box[x, k : k + 1, :] = jnp.where(within < count_tgt[at_tgt], g_here[k : k + 1, :] + norm, 0.0)
    for d in OVER_X:
        remote(g_box.at[x], g_box.at[x], g_sems.at[0], g_sems.at[1], d).start()

    f_copy.wait_recv()
    f_here = f_box[jnp.where(half == c, 0, 1), lax.rem(x, 2)]
    block = x_own[...]
    norms = jnp.sum(block * block, axis=0, keepdims=True)
    count_here = count_src[at_src]
    lane = lax.broadcasted_iota(jnp.int32, (1, LANES), 1)
    for b in range(4):
        value = f_here[b : b + 1, :] * (1.0 / SCALE) + norms[:, b * LANES : (b + 1) * LANES]
        f_out[:, b * LANES : (b + 1) * LANES] = jnp.where(b * LANES + lane < count_here, value, 0.0)

    some = num_in.at[pl.ds(0, Z_CHIPS - 1)]
    num_all = remote(some, some, num_sems.at[0], num_sems.at[1], OVER_Z_CORE[0])
    num_all.wait_recv()
    parts = [num_in.at[r] for r in range(Z_CHIPS - 1)] + [num_send.at[Z_CHIPS - 1]]
    weigh = [p[DIMS : DIMS + 1, :] for p in parts]
    total = log_sum(weigh)
    acc = jnp.zeros((DIMS, LANES), jnp.float32)
    for p, w in zip(parts, weigh):
        acc += p[0:DIMS, :] * jnp.exp2(w - total)
    anc_out[...] = jnp.where(at_src * LANES + lane < count_tgt[at_tgt], acc, 0.0)

    g_some = remote(g_box.at[pl.ds(0, 3)], g_box.at[pl.ds(0, 3)], g_sems.at[0], g_sems.at[1], OVER_X[0])
    g_some.wait_recv()
    for k in range(Z_CHIPS):
        for i in range(X_CHIPS):
            b = k * X_CHIPS + i
            g_out[:, b * LANES : (b + 1) * LANES] = g_box[i, k : k + 1, :]

    num_all.wait_send()
    g_some.wait_send()
    f_copy.wait_send()
    y_copy.wait_send()
    flag_all.wait_send()
    pair_copy.wait_send()
    remote(num_give, num_got, give_send, give_recv.at[0], OTHER_CORE).wait_send()

    @pl.when(half == c)
    def _():
        for copy in x_copies:
            copy.wait_send()

    def sent(it, _):
        row_all(it, 0).wait_send()
        row_all(it, 1).wait_send()
        return 0

    lax.fori_loop(0, ITERS, sent, 0)
    for it in range(ITERS):
        col_all(it, len(OVER_Z_CORE) if it < last else other).wait_send()


def shards(sources, targets, pair_active, count_src, count_tgt):
    f32, bf16 = jnp.float32, jnp.bfloat16
    vmem, sem = pltpu.VMEM, pltpu.SemaphoreType.DMA
    in_vmem = pl.BlockSpec(memory_space=pltpu.VMEM)
    in_smem = pl.BlockSpec(memory_space=pltpu.SMEM)
    in_place = pl.BlockSpec(memory_space=pl.ANY)
    f, g, anc = pl.pallas_call(
        kernel,
        out_shape=(
            jax.ShapeDtypeStruct((1, 512), f32),
            jax.ShapeDtypeStruct((1, 4096), f32),
            jax.ShapeDtypeStruct((DIMS, LANES), f32),
        ),
        in_specs=[in_smem, in_smem, in_smem, in_place, in_place],
        out_specs=(in_vmem, in_vmem, in_vmem),
        scratch_shapes=[
            vmem((DIMS, 512), f32),
            vmem((X_CHIPS * CORES, 1, LANES), f32),
            vmem((2, DIMS, 512), f32),
            vmem((CORES, DIMS, COLS // 2), f32),
            vmem((PAD, ROWS), f32),
            vmem((PAD, COLS), f32),
            vmem((6 * PAD + EXTRA, ROWS), bf16),
            vmem((ROWS, 6 * PAD + EXTRA), bf16),
            vmem((6 * PAD + EXTRA, COLS), bf16),
            vmem((2 * PAD, ROWS), bf16),
            vmem((COL_BLOCKS, 1, LANES), f32),
            vmem((ROWS, COLS), f32),
            vmem((ROWS, LANES), f32),
            vmem((ROWS, LANES), f32),
            vmem((ROWS, LANES), f32),
            vmem((COL_BLOCKS, 8, LANES), f32),
            vmem((COL_BLOCKS, 8, LANES), f32),
            vmem((COL_BLOCKS, 8, LANES), f32),
            vmem((ITERS, 2, 16, 4, LANES), f32),
            vmem((ITERS, 16, COL_BLOCKS, LANES), f32),
            vmem((2, 2, 4, LANES), f32),
            vmem((X_CHIPS, Z_CHIPS, LANES), f32),
            vmem((Z_CHIPS, 56, LANES), f32),
            vmem((Z_CHIPS, 56, LANES), f32),
            vmem((Z_CHIPS, 56, LANES), f32),
            vmem((Z_CHIPS, 56, LANES), f32),
            vmem((Z_CHIPS, 56, LANES), f32),
            sem((1 + Z_CHIPS,)), sem((2,)), sem(()), sem((2,)), sem((2,)), sem((ITERS, 2)), sem((ITERS, 2)),
            sem((ITERS,)), sem((ITERS,)), sem((2,)), sem((2,)), sem((2,)), sem(()), sem((Z_CHIPS,)), sem((2,)),
        ],
        compiler_params=pltpu.CompilerParams(
            collective_id=0, has_side_effects=True, vmem_limit_bytes=40 * 2**20
        ),
    )(count_src, count_tgt, pair_active, sources, targets)
    return f.reshape(512), g.reshape(4096), anc


def solution(mesh):
    return jax.shard_map(
        shards,
        mesh=mesh,
        in_specs=(P(None, "src"), P(None, "tgt"), P("src", "tgt"), P(), P()),
        out_specs=(P("src"), P("tgt"), P(None, ("tgt", "src"))),
        check_vma=False,
    )
```

```python
import math

import jax
import jax.numpy as jnp
from jax import lax
from jax.experimental import pallas as pl
from jax.experimental.pallas import tpu as pltpu
from jax.sharding import PartitionSpec as P

ITERS = 4
EPS = 0.02
SCALE = math.log2(math.e) / EPS
NEG = -(2.0**100)
LOW = -3.0e38
LOGICAL = pl.DeviceIdType.LOGICAL

DIMS = 50
PAD = 64
EXTRA = 16
ROWS = 1024
COLS = 2048
LANES = 128
COL_BLOCKS = COLS // LANES
PARTS = 2
PART_BLOCKS = ROWS // LANES // PARTS
PART_ROWS = ROWS // PARTS
X_CHIPS = 4
Y_CHIPS = 4
Z_CHIPS = 8
CORES = 2

OVER_XY = sorted(
    [(0, dx, dy, 0) for dx in range(X_CHIPS) for dy in range(Y_CHIPS) if dx or dy],
    key=lambda d: -(min(d[1], X_CHIPS - d[1]) + min(d[2], Y_CHIPS - d[2])),
)
OVER_Z = sorted([(dz, 0, 0, 0) for dz in range(1, Z_CHIPS)], key=lambda d: -min(d[0], Z_CHIPS - d[0]))
OVER_X_CORE = [(0, dx, 0, dc) for dx in range(X_CHIPS) for dc in range(CORES) if dx or dc]
OVER_X = [(0, 2, 0, 0), (0, 1, 0, 0), (0, 3, 0, 0)]
OTHER_CORE = (0, 0, 0, 1)
PARTNERS = OVER_XY + OVER_Z + [OTHER_CORE] + [d for d in OVER_X_CORE if d[1] and d[3]]


def tree(op, parts):
    while len(parts) > 1:
        parts = [op(*parts[i : i + 2]) if i + 1 < len(parts) else parts[i] for i in range(0, len(parts), 2)]
    return parts[0]


def log_sum(parts):
    peak = tree(jnp.maximum, parts)
    total = tree(jnp.add, [jnp.exp2(p - peak) for p in parts])
    return peak + jnp.log2(total)


def split(value, pieces):
    out = []
    for _ in range(pieces):
        piece = value.astype(jnp.bfloat16)
        out.append(piece)
        value = value - piece.astype(jnp.float32)
    return out


def kernel(
    counts_src, counts_tgt, pairs, src, tgt,
    f_out, g_out, anc_out,
    count_src, count_tgt, pair, x_own, flags, x_in, y_in, x_full, y_full, y_stack, x_pieces, y_norms,
    logits, row_peak, row_total, f_rep, g_rep, col_peak, col_total,
    row_box, col_box, core_box, f_box, g_box, num_own, num_give, num_got, num_send, num_in,
    own_sems, flag_sems, x_send, x_recv, y_sems, row_send, row_recv, col_send, col_recv, core_send, core_recv, f_sems, g_sems,
    give_send, give_recv, num_sems,
):
    at_src = lax.axis_index("src")
    at_tgt = lax.axis_index("tgt")
    z, x = at_src // X_CHIPS, at_src & (X_CHIPS - 1)
    y, c = at_tgt // CORES, at_tgt & (CORES - 1)
    half = x // 2

    def device(d):
        dz, dx, dy, dc = d
        at_z = (z + dz) & (Z_CHIPS - 1) if not isinstance(dz, int) or dz else z
        at_x = (x + dx) & (X_CHIPS - 1) if dx else x
        at_y = (y + dy) & (Y_CHIPS - 1) if dy else y
        at_c = c ^ dc
        return ((at_z * X_CHIPS + at_x) * Y_CHIPS + at_y) * CORES + at_c

    ids = {d: device(d) for d in PARTNERS}

    def remote(a, b, send, recv, d):
        return pltpu.make_async_remote_copy(
            src_ref=a, dst_ref=b, send_sem=send, recv_sem=recv, device_id=ids[d] if isinstance(d[0], int) else device(d), device_id_type=LOGICAL
        )

    def lanes(k, width=LANES):
        return pl.ds(pl.multiple_of(k * width, width), width)

    barrier = pltpu.get_barrier_semaphore()
    for d in PARTNERS:
        pl.semaphore_signal(barrier, inc=1, device_id=ids[d], device_id_type=LOGICAL)

    x_local = [pltpu.make_async_copy(src.at[:, lanes(k)], x_own.at[k], own_sems.at[k]) for k in range(4)]
    for copy in x_local:
        copy.start()
    y_local = [
        pltpu.make_async_copy(tgt.at[:, lanes(k * X_CHIPS + x)], y_in.at[c, :, lanes(k)], own_sems.at[4 + k])
        for k in range(Z_CHIPS)
    ]
    for copy in y_local:
        copy.start()
    scalars = [
        pltpu.make_async_copy(a, b, own_sems.at[4 + Z_CHIPS + i])
        for i, (a, b) in enumerate(((counts_src, count_src), (counts_tgt, count_tgt), (pairs, pair)))
    ]
    for copy in scalars:
        copy.start()
    for copy in scalars:
        copy.wait()
    mine = x * CORES + c
    listed = (pair[0, 0] > 0).astype(jnp.float32)
    flags[mine] = jnp.full((1, LANES), listed, jnp.float32)
    for copy in x_local + y_local:
        copy.wait()
    pl.semaphore_wait(barrier, len(PARTNERS))

    x_copies = [
        remote(x_own.at[k], x_in.at[x & 1, k], x_send, x_recv.at[x & 1, k], d) for k in range(4) for d in OVER_X
    ]

    @pl.when(half == c)
    def _():
        for copy in x_copies:
            copy.start()

    y_copy = remote(y_in.at[c], y_in.at[c], y_sems.at[0], y_sems.at[1], OTHER_CORE)
    y_copy.start()
    for d in OVER_X_CORE:
        remote(flags.at[mine], flags.at[mine], flag_sems.at[0], flag_sems.at[1], d).start()

    def number_of(counts, length):
        total = counts[0]
        for i in range(1, length):
            total = total + counts[i]
        return total.astype(jnp.float32)

    log_a = -jnp.log2(jnp.full((PART_BLOCKS, LANES), number_of(count_src, Z_CHIPS * X_CHIPS), jnp.float32))
    log_b = -jnp.log2(jnp.full((Z_CHIPS, LANES), number_of(count_tgt, Y_CHIPS * CORES), jnp.float32))
    col_counts = [count_tgt[y * CORES + i] for i in range(CORES)]

    def places(shape):
        return lax.broadcasted_iota(jnp.int32, shape, 0), lax.broadcasted_iota(jnp.int32, shape, 1)

    def row_live(q):
        block, lane = places((PART_BLOCKS, LANES))
        within = (lax.rem(q * PART_BLOCKS, 4) + block) * LANES + lane
        return within < count_src[z * X_CHIPS + 2 * c + q * PART_BLOCKS // 4]

    block, lane = places((Z_CHIPS, LANES))
    col_within = (block * X_CHIPS + x) * LANES + lane
    col_live = [col_within < count for count in col_counts]

    x_full[DIMS:PAD, :] = jnp.zeros((PAD - DIMS, ROWS), jnp.float32)
    y_full[DIMS:PAD, :] = jnp.zeros((PAD - DIMS, COLS), jnp.float32)

    def columns_of(tile):
        y_full[0:DIMS, lanes(tile, COLS // 2)] = y_in[tile]

        def body(k, _):
            b = tile * Z_CHIPS + k
            whole = y_full[:, lanes(b)]
            norm = jnp.sum(whole * whole, axis=0, keepdims=True)
            y_norms[b] = norm
            g_rep[b] = jnp.broadcast_to(-SCALE * norm, (8, LANES))
            p1, p2, p3 = split(whole, 3)
            for i, p in enumerate((p1, p2, p1, p3, p1, p2)):
                y_stack[i * PAD : (i + 1) * PAD, lanes(b)] = p
            return 0

        lax.fori_loop(0, Z_CHIPS, body, 0)

    columns_of(c)
    y_copy.wait_recv()
    columns_of(1 - c)
    flag_some = flags.at[pl.ds(0, len(OVER_X_CORE))]
    flag_all = remote(flag_some, flag_some, flag_sems.at[0], flag_sems.at[1], OTHER_CORE)
    flag_all.wait_recv()
    line, lane = places((EXTRA, LANES))
    for b in range(COL_BLOCKS):
        tile, k = b // Z_CHIPS, b % Z_CHIPS
        dead = jnp.where((k * X_CHIPS + x) * LANES + lane < col_counts[tile], 0.0, NEG)
        rows = [jnp.minimum(jnp.where(flags[(2 * c + i) * CORES + tile] > 0, 0.0, NEG), dead) for i in range(2)]
        extra = jnp.where(line == 0, rows[0], jnp.where(line == 1, rows[1], jnp.where(line == 2, 1.0, 0.0)))
        y_stack[6 * PAD :, b * LANES : (b + 1) * LANES] = extra.astype(jnp.bfloat16)

    def rows_of(h, k):
        live = count_src[z * X_CHIPS + 2 * c + h]
        at = lanes(4 * h + k)
        x_full[0:DIMS, at] = x_in[h, k]
        whole = x_full[:, at]
        q1, q2 = split(whole, 2)
        x_pieces[0:PAD, at] = q1
        x_pieces[PAD:, at] = q2
        p1, p2, p3 = split(whole * (2.0 * SCALE), 3)
        dead = jnp.where(k * LANES + lane < live, 0.0, NEG)
        extra = jnp.where(line == 2, dead, jnp.where(line == h, 1.0, 0.0))
        stack = jnp.concatenate([p1, p1, p2, p1, p3, p2, extra.astype(jnp.bfloat16)], axis=0)
        rows = stack.T
        for i in range(COLS // 256):
            cols = slice(i * 256, (i + 1) * 256)
            logits[at, cols] = jnp.dot(rows, y_stack[:, cols], preferred_element_type=jnp.float32)

    def row_all(it, q):
        some = row_box.at[it, q, pl.ds(0, len(OVER_XY))]
        return remote(some, some, row_send.at[it, q], row_recv.at[it, q], OVER_XY[0])

    def row_sums_at(base, tile):
        g = [g_rep[tile * 8 + b] for b in range(8)]
        for i in range(16):
            at = pl.ds(pl.multiple_of(base + 8 * i, 8), 8)
            parts = [logits[at, (tile * 8 + b) * LANES : (tile * 8 + b + 1) * LANES] + g[b] for b in range(8)]
            best = tree(jnp.maximum, parts)
            if tile:
                peak = row_peak[at, :]
                best = jnp.maximum(best, peak)
            total = tree(jnp.add, [jnp.exp2(p - best) for p in parts])
            if tile:
                total += row_total[at, :] * jnp.exp2(peak - best)
            row_peak[at, :] = best
            row_total[at, :] = total

    def row_sums(q, tile):
        def body(k, _):
            row_sums_at(q * PART_ROWS + k * LANES, tile)
            return 0

        lax.fori_loop(0, PART_BLOCKS, body, 0)

    def row_start(it, q):
        own = row_box.at[it, q, len(OVER_XY)]
        for b in range(PART_BLOCKS):
            peaks = row_peak[lanes(PART_BLOCKS * q + b), :].T
            totals = row_total[lanes(PART_BLOCKS * q + b), :].T
            peak = jnp.max(peaks, axis=0, keepdims=True)
            total = jnp.sum(totals * jnp.exp2(peaks - peak), axis=0, keepdims=True)
            own[b : b + 1, :] = peak + jnp.log2(total)
        for r, d in enumerate(OVER_XY):
            remote(own, row_box.at[it, q, r], row_send.at[it, q], row_recv.at[it, q], d).start()

    def row_end(it, q):
        row_all(it, q).wait_recv()
        total = log_sum([row_box[it, q, r] for r in range(len(OVER_XY) + 1)])
        f = jnp.where(row_live(q), log_a - total, 0.0)
        for b in range(PART_BLOCKS):
            f_rep[lanes(PART_BLOCKS * q + b), :] = jnp.broadcast_to(f[b : b + 1, :], (LANES, LANES)).T
        return f

    def col_sums(q, tiles):
        def body(k, _):
            base = q * PART_ROWS + k * 64
            f = [f_rep[pl.ds(pl.multiple_of(base + 8 * j, 8), 8), :] for j in range(8)]
            for tile in tiles:
                for b in range(tile * 8, tile * 8 + 8):
                    parts = [
                        logits[pl.ds(pl.multiple_of(base + 8 * j, 8), 8), b * LANES : (b + 1) * LANES] + f[j]
                        for j in range(8)
                    ]
                    peak = col_peak[b]
                    best = jnp.maximum(peak, tree(jnp.maximum, parts))
                    fresh = tree(jnp.add, [jnp.exp2(p - best) for p in parts])
                    col_total[b] = col_total[b] * jnp.exp2(peak - best) + fresh
                    col_peak[b] = best
            return 0

        lax.fori_loop(0, PART_ROWS // 64, body, 0, unroll=4)

    def col_reset():
        col_peak[...] = jnp.full((COL_BLOCKS, 8, LANES), LOW, jnp.float32)
        col_total[...] = jnp.zeros((COL_BLOCKS, 8, LANES), jnp.float32)

    def col_sum(tile):
        peaks = col_peak[tile * 8 : tile * 8 + 8]
        peak = jnp.max(peaks, axis=1, keepdims=True)
        total = jnp.sum(col_total[tile * 8 : tile * 8 + 8] * jnp.exp2(peaks - peak), axis=1)
        return peak[:, 0, :] + jnp.log2(total)

    def col_give(it, tile, value):
        own = col_box.at[it, tile, len(OVER_Z)]
        own[...] = value
        for r, d in enumerate(OVER_Z):
            remote(own, col_box.at[it, tile, r], col_send.at[it, tile], col_recv.at[it, tile], d).start()

    def col_all(it, tile):
        some = col_box.at[it, tile, pl.ds(0, len(OVER_Z))]
        return remote(some, some, col_send.at[it, tile], col_recv.at[it, tile], OVER_Z[0])

    def over_z(it, tile):
        col_all(it, tile).wait_recv()
        return log_sum([col_box[it, tile, r] for r in range(len(OVER_Z) + 1)])

    def core_copy(it, tile):
        return remote(
            core_box.at[it, tile, 1], core_box.at[it, tile, 0], core_send.at[it, tile], core_recv.at[it, tile], OTHER_CORE
        )

    def core_give(it, tile, value):
        core_box[it, tile, 1] = value
        core_copy(it, tile).start()

    def over_cores(it, tile):
        core_copy(it, tile).wait_recv()
        return log_sum([core_box[it, tile, r] for r in range(2)])

    for i in range(2):
        h = (x & 1) ^ jnp.where(half == c, i, 1 - i)
        here = x == 2 * c + h

        @pl.when(here)
        def _():
            x_in[h] = x_own[...]

        def rows_and_sums(k, _):
            @pl.when(jnp.logical_not(here))
            def _():
                remote(x_in.at[h, k], x_in.at[h, k], x_send, x_recv.at[h, k], OVER_X[0]).wait_recv()

            rows_of(h, k)
            for tile in range(CORES):
                row_sums_at((4 * h + k) * LANES, tile)
            return 0

        lax.fori_loop(0, 4, rows_and_sums, 0)
        row_start(0, h)

    def columns_from_rows(it, give):
        col_reset()
        for q in range(PARTS):
            f_box[0, q] = row_end(it, q)
            if q < PARTS - 1:
                col_sums(q, (0, 1))
        for tile in range(CORES):
            col_sums(PARTS - 1, (tile,))
            give(it, tile, col_sum(tile))

    def iteration(it, _):
        columns_from_rows(it, col_give)
        for tile in range(CORES):
            core_give(it, tile, over_z(it, tile))
        for tile in range(CORES):
            g = jnp.where(col_live[tile], log_b - over_cores(it, tile), 0.0)
            for b in range(Z_CHIPS):
                g_rep[tile * Z_CHIPS + b] = jnp.broadcast_to(g[b : b + 1, :], (8, LANES))
            for q in range(PARTS):
                row_sums(q, tile)
                if tile == CORES - 1:
                    row_start(it + 1, q)
        return 0

    last = ITERS - 1
    lax.fori_loop(0, last, iteration, 0)
    columns_from_rows(last, core_give)
    f_copy = remote(f_box.at[0], f_box.at[1], f_sems.at[0], f_sems.at[1], OTHER_CORE)
    f_copy.start()
    both = [over_cores(last, tile) for tile in range(CORES)]
    col_give(last, 0, jnp.where(c == 0, both[0], both[1]))
    for tile in range(CORES):
        for b in range(Z_CHIPS):
            col_peak[tile * Z_CHIPS + b] = jnp.broadcast_to(both[tile][b : b + 1, :], (8, LANES))

    def distance(k):
        step = (k + 1) // 2
        return jnp.where(lax.rem(k, 2) == 0, 4 + step, 4 - step)

    def give(k):
        return remote(num_give.at[k], num_got.at[k], give_send, give_recv.at[k], OTHER_CORE)

    def ancestors_of(k, _):
        @pl.when(k < Z_CHIPS)
        def _():
            to = lax.rem(z + distance(k), Z_CHIPS)
            cols = [lanes(i * Z_CHIPS + to) for i in range(CORES)]
            local = [col_peak[i * Z_CHIPS + to] for i in range(CORES)]
            acc = jnp.zeros((PAD, CORES * LANES), jnp.float32)
            for r in range(ROWS // 256):
                at = slice(r * 256, (r + 1) * 256)
                f = f_rep[at, :]
                weight = jnp.concatenate(
                    [jnp.exp2(logits[at, cols[i]] + (f - local[i][0:1, :])) for i in range(CORES)], axis=1
                )
                w1, w2 = split(weight, 2)
                two = jnp.dot(x_pieces[:, at], w1, preferred_element_type=jnp.float32)
                acc += two[0:PAD] + two[PAD:] + jnp.dot(x_pieces[0:PAD, at], w2, preferred_element_type=jnp.float32)
            tiles = [acc[0:56, i * LANES : (i + 1) * LANES] for i in range(CORES)]
            num_own[k] = jnp.where(c == 0, tiles[0], tiles[1])
            num_give[k] = jnp.where(c == 0, tiles[1], tiles[0])
            give(k).start()

        @pl.when(k >= 2)
        def _():
            j = k - 2
            dz = distance(j)
            give(j).wait_recv()
            num_send[j] = num_own[j] + num_got[j]
            num_send[j, DIMS : DIMS + 1, :] = col_peak[c * Z_CHIPS + lax.rem(z + dz, Z_CHIPS)][0:1, :]

            @pl.when(j < Z_CHIPS - 1)
            def _():
                remote(num_send.at[j], num_in.at[j], num_sems.at[0], num_sems.at[1], (dz, 0, 0, 0)).start()

        return 0

    lax.fori_loop(0, Z_CHIPS + 2, ancestors_of, 0)

    live_here = col_within < count_tgt[at_tgt]
    g_here = jnp.where(live_here, (log_b - over_z(last, 0)) * (1.0 / SCALE), 0.0)
    for k in range(Z_CHIPS):
        norm = y_norms[c * Z_CHIPS + k]
        within = (k * X_CHIPS + x) * LANES + lax.broadcasted_iota(jnp.int32, (1, LANES), 1)
        g_box[x, k : k + 1, :] = jnp.where(within < count_tgt[at_tgt], g_here[k : k + 1, :] + norm, 0.0)
    for d in OVER_X:
        remote(g_box.at[x], g_box.at[x], g_sems.at[0], g_sems.at[1], d).start()

    f_copy.wait_recv()
    count_here = count_src[at_src]
    lane = lax.broadcasted_iota(jnp.int32, (1, LANES), 1)
    from_core = jnp.where(half == c, 0, 1)
    for b in range(4):
        at = lax.rem(x, 2) * 4 + b
        f_here = f_box[from_core, at // PART_BLOCKS, lax.rem(at, PART_BLOCKS)]
        value = f_here[None, :] * (1.0 / SCALE) + jnp.sum(x_own[b] * x_own[b], axis=0, keepdims=True)
        f_out[:, b * LANES : (b + 1) * LANES] = jnp.where(b * LANES + lane < count_here, value, 0.0)

    some = num_in.at[pl.ds(0, Z_CHIPS - 1)]
    num_all = remote(some, some, num_sems.at[0], num_sems.at[1], OVER_Z[0])
    num_all.wait_recv()
    parts = [num_in.at[r] for r in range(Z_CHIPS - 1)] + [num_send.at[Z_CHIPS - 1]]
    weigh = [p[DIMS : DIMS + 1, :] for p in parts]
    total = log_sum(weigh)
    acc = jnp.zeros((DIMS, LANES), jnp.float32)
    for p, w in zip(parts, weigh):
        acc += p[0:DIMS, :] * jnp.exp2(w - total)
    anc_out[...] = jnp.where(at_src * LANES + lane < count_tgt[at_tgt], acc, 0.0)

    g_some = remote(g_box.at[pl.ds(0, 3)], g_box.at[pl.ds(0, 3)], g_sems.at[0], g_sems.at[1], OVER_X[0])
    g_some.wait_recv()
    for k in range(Z_CHIPS):
        for i in range(X_CHIPS):
            b = k * X_CHIPS + i
            g_out[:, b * LANES : (b + 1) * LANES] = g_box[i, k : k + 1, :]

    num_all.wait_send()
    g_some.wait_send()
    f_copy.wait_send()
    y_copy.wait_send()
    flag_all.wait_send()
    remote(num_give, num_got, give_send, give_recv.at[0], OTHER_CORE).wait_send()

    @pl.when(half == c)
    def _():
        for copy in x_copies:
            copy.wait_send()

    def sent(it, _):
        for q in range(PARTS):
            row_all(it, q).wait_send()
        return 0

    lax.fori_loop(0, ITERS, sent, 0)
    for it in range(ITERS):
        for tile in range(CORES):
            core_copy(it, tile).wait_send()
            if it < last or tile == 0:
                col_all(it, tile).wait_send()


def hand_over(f, g, anc, f_out, g_out, anc_out, sems):
    copies = [
        pltpu.make_async_copy(a, b, sems.at[i]) for i, (a, b) in enumerate(((f, f_out), (g, g_out), (anc, anc_out)))
    ]
    for copy in copies:
        copy.start()
    for copy in copies:
        copy.wait()


def in_hbm_now(array):
    return pltpu.with_memory_space_constraint(array, pltpu.HBM)


def shards(sources, targets, pair_active, count_src, count_tgt):
    f32, bf16 = jnp.float32, jnp.bfloat16
    vmem, sem = pltpu.VMEM, pltpu.SemaphoreType.DMA
    in_vmem = pl.BlockSpec(memory_space=pltpu.VMEM)
    in_hbm = pl.BlockSpec(memory_space=pltpu.HBM)
    f, g, anc = pl.pallas_call(
        kernel,
        out_shape=(
            jax.ShapeDtypeStruct((1, 512), f32),
            jax.ShapeDtypeStruct((1, 4096), f32),
            jax.ShapeDtypeStruct((DIMS, LANES), f32),
        ),
        in_specs=[in_hbm] * 5,
        out_specs=(in_vmem, in_vmem, in_vmem),
        scratch_shapes=[
            pltpu.SMEM((32,), jnp.int32),
            pltpu.SMEM((8,), jnp.int32),
            pltpu.SMEM((1, 1), jnp.int32),
            vmem((4, DIMS, LANES), f32),
            vmem((X_CHIPS * CORES, 1, LANES), f32),
            vmem((2, 4, DIMS, LANES), f32),
            vmem((CORES, DIMS, COLS // 2), f32),
            vmem((PAD, ROWS), f32),
            vmem((PAD, COLS), f32),
            vmem((6 * PAD + EXTRA, COLS), bf16),
            vmem((2 * PAD, ROWS), bf16),
            vmem((COL_BLOCKS, 1, LANES), f32),
            vmem((ROWS, COLS), f32),
            vmem((ROWS, LANES), f32),
            vmem((ROWS, LANES), f32),
            vmem((ROWS, LANES), f32),
            vmem((COL_BLOCKS, 8, LANES), f32),
            vmem((COL_BLOCKS, 8, LANES), f32),
            vmem((COL_BLOCKS, 8, LANES), f32),
            vmem((ITERS, PARTS, 16, PART_BLOCKS, LANES), f32),
            vmem((ITERS, CORES, Z_CHIPS, Z_CHIPS, LANES), f32),
            vmem((ITERS, CORES, 2, Z_CHIPS, LANES), f32),
            vmem((2, PARTS, PART_BLOCKS, LANES), f32),
            vmem((X_CHIPS, Z_CHIPS, LANES), f32),
            vmem((Z_CHIPS, 56, LANES), f32),
            vmem((Z_CHIPS, 56, LANES), f32),
            vmem((Z_CHIPS, 56, LANES), f32),
            vmem((Z_CHIPS, 56, LANES), f32),
            vmem((Z_CHIPS, 56, LANES), f32),
            sem((7 + Z_CHIPS,)), sem((2,)), sem(()), sem((2, 4)), sem((2,)), sem((ITERS, PARTS)), sem((ITERS, PARTS)),
            sem((ITERS, 2)), sem((ITERS, 2)), sem((ITERS, 2)), sem((ITERS, 2)), sem((2,)), sem((2,)),
            sem(()), sem((Z_CHIPS,)), sem((2,)),
        ],
        compiler_params=pltpu.CompilerParams(
            collective_id=0, has_side_effects=True, vmem_limit_bytes=40 * 2**20
        ),
    )(in_hbm_now(count_src), in_hbm_now(count_tgt), pair_active, in_hbm_now(sources), in_hbm_now(targets))
    f, g, anc = pl.pallas_call(
        hand_over,
        out_shape=(
            jax.ShapeDtypeStruct((1, 512), f32),
            jax.ShapeDtypeStruct((1, 4096), f32),
            jax.ShapeDtypeStruct((DIMS, LANES), f32),
        ),
        in_specs=[pl.BlockSpec(memory_space=pl.ANY)] * 3,
        out_specs=(in_hbm,) * 3,
        scratch_shapes=[sem((3,))],
        compiler_params=pltpu.CompilerParams(vmem_limit_bytes=40 * 2**20),
    )(f, g, anc)
    return f.reshape(512), g.reshape(4096), anc


def solution(mesh):
    return jax.shard_map(
        shards,
        mesh=mesh,
        in_specs=(P(None, "src"), P(None, "tgt"), P("src", "tgt"), P(), P()),
        out_specs=(P("src"), P("tgt"), P(None, ("tgt", "src"))),
        check_vma=False,
    )
```

```python
import math

import jax
import jax.numpy as jnp
from jax import lax
from jax.experimental import pallas as pl
from jax.experimental.pallas import tpu as pltpu
from jax.sharding import PartitionSpec as P

ITERS = 4
EPS = 0.02
SCALE = math.log2(math.e) / EPS
NEG = -(2.0**100)
LOW = -3.0e38
LOGICAL = pl.DeviceIdType.LOGICAL

DIMS = 50
PAD = 64
EXTRA = 16
ROWS = 1024
COLS = 2048
LANES = 128
COL_BLOCKS = COLS // LANES
PARTS = 2
PART_BLOCKS = ROWS // LANES // PARTS
PART_ROWS = ROWS // PARTS
X_CHIPS = 4
Y_CHIPS = 4
Z_CHIPS = 8
CORES = 2

OVER_XY = sorted(
    [(0, dx, dy, 0) for dx in range(X_CHIPS) for dy in range(Y_CHIPS) if dx or dy],
    key=lambda d: -(min(d[1], X_CHIPS - d[1]) + min(d[2], Y_CHIPS - d[2])),
)
OVER_Z = sorted([(dz, 0, 0, 0) for dz in range(1, Z_CHIPS)], key=lambda d: -min(d[0], Z_CHIPS - d[0]))
OVER_X_CORE = [(0, dx, 0, dc) for dx in range(X_CHIPS) for dc in range(CORES) if dx or dc]
OVER_X = [(0, 2, 0, 0), (0, 1, 0, 0), (0, 3, 0, 0)]
OTHER_CORE = (0, 0, 0, 1)
PARTNERS = OVER_XY + OVER_Z + [OTHER_CORE] + [d for d in OVER_X_CORE if d[1] and d[3]]


def tree(op, parts):
    while len(parts) > 1:
        parts = [op(*parts[i : i + 2]) if i + 1 < len(parts) else parts[i] for i in range(0, len(parts), 2)]
    return parts[0]


def log_sum(parts):
    peak = tree(jnp.maximum, parts)
    total = tree(jnp.add, [jnp.exp2(p - peak) for p in parts])
    return peak + jnp.log2(total)


def split(value, pieces):
    out = []
    for _ in range(pieces):
        piece = value.astype(jnp.bfloat16)
        out.append(piece)
        value = value - piece.astype(jnp.float32)
    return out


def kernel(
    counts_src, counts_tgt, pairs, src, tgt,
    f_out, g_out, anc_out,
    count_src, count_tgt, pair, x_own, flags, x_in, y_in, x_full, y_full, y_stack, x_pieces, y_norms,
    logits, row_peak, row_total, f_rep, g_rep, col_peak, col_total,
    row_box, col_box, core_box, g_sum_box, f_box, g_box, num_own, num_give, num_got, num_send, num_in,
    own_sems, flag_sems, x_send, x_recv, y_sems, row_send, row_recv, col_send, col_recv, core_send, core_recv, g_sum_sems, f_sems, g_sems,
    give_send, give_recv, num_sems,
):
    at_src = lax.axis_index("src")
    at_tgt = lax.axis_index("tgt")
    z, x = at_src // X_CHIPS, at_src & (X_CHIPS - 1)
    y, c = at_tgt // CORES, at_tgt & (CORES - 1)
    half = x // 2

    def device(d):
        dz, dx, dy, dc = d
        at_z = (z + dz) & (Z_CHIPS - 1) if not isinstance(dz, int) or dz else z
        at_x = (x + dx) & (X_CHIPS - 1) if dx else x
        at_y = (y + dy) & (Y_CHIPS - 1) if dy else y
        at_c = c ^ dc
        return ((at_z * X_CHIPS + at_x) * Y_CHIPS + at_y) * CORES + at_c

    ids = {d: device(d) for d in PARTNERS}

    def remote(a, b, send, recv, d):
        return pltpu.make_async_remote_copy(
            src_ref=a, dst_ref=b, send_sem=send, recv_sem=recv, device_id=ids[d] if isinstance(d[0], int) else device(d), device_id_type=LOGICAL
        )

    def lanes(k, width=LANES):
        return pl.ds(pl.multiple_of(k * width, width), width)

    barrier = pltpu.get_barrier_semaphore()
    for d in PARTNERS:
        pl.semaphore_signal(barrier, inc=1, device_id=ids[d], device_id_type=LOGICAL)

    x_local = [pltpu.make_async_copy(src.at[:, lanes(k)], x_own.at[k], own_sems.at[k]) for k in range(4)]
    for copy in x_local:
        copy.start()
    y_local = [
        pltpu.make_async_copy(tgt.at[:, lanes(k * X_CHIPS + x)], y_in.at[c, :, lanes(k)], own_sems.at[4 + k])
        for k in range(Z_CHIPS)
    ]
    for copy in y_local:
        copy.start()
    scalars = [
        pltpu.make_async_copy(a, b, own_sems.at[4 + Z_CHIPS + i])
        for i, (a, b) in enumerate(((counts_src, count_src), (counts_tgt, count_tgt), (pairs, pair)))
    ]
    for copy in scalars:
        copy.start()
    for copy in scalars:
        copy.wait()
    mine = x * CORES + c
    listed = (pair[0, 0] > 0).astype(jnp.float32)
    flags[mine] = jnp.full((1, LANES), listed, jnp.float32)
    for copy in x_local + y_local:
        copy.wait()
    pl.semaphore_wait(barrier, len(PARTNERS))

    x_copies = [
        remote(x_own.at[k], x_in.at[x & 1, k], x_send, x_recv.at[x & 1, k], d) for k in range(4) for d in OVER_X
    ]

    @pl.when(half == c)
    def _():
        for copy in x_copies:
            copy.start()

    y_copy = remote(y_in.at[c], y_in.at[c], y_sems.at[0], y_sems.at[1], OTHER_CORE)
    y_copy.start()
    for d in OVER_X_CORE:
        remote(flags.at[mine], flags.at[mine], flag_sems.at[0], flag_sems.at[1], d).start()

    def number_of(counts, length):
        total = counts[0]
        for i in range(1, length):
            total = total + counts[i]
        return total.astype(jnp.float32)

    log_a = -jnp.log2(jnp.full((PART_BLOCKS, LANES), number_of(count_src, Z_CHIPS * X_CHIPS), jnp.float32))
    log_b = -jnp.log2(jnp.full((COL_BLOCKS, LANES), number_of(count_tgt, Y_CHIPS * CORES), jnp.float32))
    col_counts = [count_tgt[y * CORES + i] for i in range(CORES)]

    def places(shape):
        return lax.broadcasted_iota(jnp.int32, shape, 0), lax.broadcasted_iota(jnp.int32, shape, 1)

    def row_live(q):
        block, lane = places((PART_BLOCKS, LANES))
        within = (lax.rem(q * PART_BLOCKS, 4) + block) * LANES + lane
        return within < count_src[z * X_CHIPS + 2 * c + q * PART_BLOCKS // 4]

    block, lane = places((Z_CHIPS, LANES))
    col_within = (block * X_CHIPS + x) * LANES + lane
    two_within = jnp.concatenate([col_within] * CORES, axis=0)
    two_block = lax.broadcasted_iota(jnp.int32, (COL_BLOCKS, LANES), 0)
    col_live = two_within < jnp.where(two_block < Z_CHIPS, col_counts[0], col_counts[1])

    x_full[DIMS:PAD, :] = jnp.zeros((PAD - DIMS, ROWS), jnp.float32)
    y_full[DIMS:PAD, :] = jnp.zeros((PAD - DIMS, COLS), jnp.float32)

    def columns_of(tile):
        y_full[0:DIMS, lanes(tile, COLS // 2)] = y_in[tile]

        def body(k, _):
            b = tile * Z_CHIPS + k
            whole = y_full[:, lanes(b)]
            norm = jnp.sum(whole * whole, axis=0, keepdims=True)
            y_norms[b] = norm
            g_rep[b] = jnp.broadcast_to(-SCALE * norm, (8, LANES))
            p1, p2, p3 = split(whole, 3)
            for i, p in enumerate((p1, p2, p1, p3, p1, p2)):
                y_stack[i * PAD : (i + 1) * PAD, lanes(b)] = p
            return 0

        lax.fori_loop(0, Z_CHIPS, body, 0)

    columns_of(c)
    y_copy.wait_recv()
    columns_of(1 - c)
    flag_some = flags.at[pl.ds(0, len(OVER_X_CORE))]
    flag_all = remote(flag_some, flag_some, flag_sems.at[0], flag_sems.at[1], OTHER_CORE)
    flag_all.wait_recv()
    line, lane = places((EXTRA, LANES))
    for b in range(COL_BLOCKS):
        tile, k = b // Z_CHIPS, b % Z_CHIPS
        dead = jnp.where((k * X_CHIPS + x) * LANES + lane < col_counts[tile], 0.0, NEG)
        rows = [jnp.minimum(jnp.where(flags[(2 * c + i) * CORES + tile] > 0, 0.0, NEG), dead) for i in range(2)]
        extra = jnp.where(line == 0, rows[0], jnp.where(line == 1, rows[1], jnp.where(line == 2, 1.0, 0.0)))
        y_stack[6 * PAD :, b * LANES : (b + 1) * LANES] = extra.astype(jnp.bfloat16)

    def rows_of(h, k):
        live = count_src[z * X_CHIPS + 2 * c + h]
        at = lanes(4 * h + k)
        x_full[0:DIMS, at] = x_in[h, k]
        whole = x_full[:, at]
        q1, q2 = split(whole, 2)
        x_pieces[0:PAD, at] = q1
        x_pieces[PAD:, at] = q2
        p1, p2, p3 = split(whole * (2.0 * SCALE), 3)
        dead = jnp.where(k * LANES + lane < live, 0.0, NEG)
        extra = jnp.where(line == 2, dead, jnp.where(line == h, 1.0, 0.0))
        stack = jnp.concatenate([p1, p1, p2, p1, p3, p2, extra.astype(jnp.bfloat16)], axis=0)
        rows = stack.T
        for i in range(COLS // 256):
            cols = slice(i * 256, (i + 1) * 256)
            logits[at, cols] = jnp.dot(rows, y_stack[:, cols], preferred_element_type=jnp.float32)

    def row_all(it, q):
        some = row_box.at[it, q, pl.ds(0, len(OVER_XY))]
        return remote(some, some, row_send.at[it, q], row_recv.at[it, q], OVER_XY[0])

    def row_sums_at(base, tile):
        g = [g_rep[tile * 8 + b] for b in range(8)]
        for i in range(16):
            at = pl.ds(pl.multiple_of(base + 8 * i, 8), 8)
            parts = [logits[at, (tile * 8 + b) * LANES : (tile * 8 + b + 1) * LANES] + g[b] for b in range(8)]
            best = tree(jnp.maximum, parts)
            if tile:
                peak = row_peak[at, :]
                best = jnp.maximum(best, peak)
            total = tree(jnp.add, [jnp.exp2(p - best) for p in parts])
            if tile:
                total += row_total[at, :] * jnp.exp2(peak - best)
            row_peak[at, :] = best
            row_total[at, :] = total

    def row_sums(q, tile):
        def body(k, _):
            row_sums_at(q * PART_ROWS + k * LANES, tile)
            return 0

        lax.fori_loop(0, PART_BLOCKS, body, 0)

    def row_start(it, q):
        own = row_box.at[it, q, len(OVER_XY)]
        for b in range(PART_BLOCKS):
            peaks = row_peak[lanes(PART_BLOCKS * q + b), :].T
            totals = row_total[lanes(PART_BLOCKS * q + b), :].T
            peak = jnp.max(peaks, axis=0, keepdims=True)
            total = jnp.sum(totals * jnp.exp2(peaks - peak), axis=0, keepdims=True)
            own[b : b + 1, :] = peak + jnp.log2(total)
        for r, d in enumerate(OVER_XY):
            remote(own, row_box.at[it, q, r], row_send.at[it, q], row_recv.at[it, q], d).start()

    def row_end(it, q):
        row_all(it, q).wait_recv()
        total = log_sum([row_box[it, q, r] for r in range(len(OVER_XY) + 1)])
        f = jnp.where(row_live(q), log_a - total, 0.0)
        for b in range(PART_BLOCKS):
            f_rep[lanes(PART_BLOCKS * q + b), :] = jnp.broadcast_to(f[b : b + 1, :], (LANES, LANES)).T
        return f

    def col_sums(q, tiles):
        def body(k, _):
            base = q * PART_ROWS + k * 64
            f = [f_rep[pl.ds(pl.multiple_of(base + 8 * j, 8), 8), :] for j in range(8)]
            for tile in tiles:
                for b in range(tile * 8, tile * 8 + 8):
                    parts = [
                        logits[pl.ds(pl.multiple_of(base + 8 * j, 8), 8), b * LANES : (b + 1) * LANES] + f[j]
                        for j in range(8)
                    ]
                    peak = col_peak[b]
                    best = jnp.maximum(peak, tree(jnp.maximum, parts))
                    fresh = tree(jnp.add, [jnp.exp2(p - best) for p in parts])
                    col_total[b] = col_total[b] * jnp.exp2(peak - best) + fresh
                    col_peak[b] = best
            return 0

        lax.fori_loop(0, PART_ROWS // 64, body, 0, unroll=4)

    def col_reset():
        col_peak[...] = jnp.full((COL_BLOCKS, 8, LANES), LOW, jnp.float32)
        col_total[...] = jnp.zeros((COL_BLOCKS, 8, LANES), jnp.float32)

    def col_total_of():
        peaks = col_peak[...]
        peak = jnp.max(peaks, axis=1, keepdims=True)
        total = jnp.sum(col_total[...] * jnp.exp2(peaks - peak), axis=1)
        return peak[:, 0, :] + jnp.log2(total)

    def over_z(box, send, recv):
        some = box.at[pl.ds(0, len(OVER_Z))]
        return remote(some, some, send, recv, OVER_Z[0])

    def give_over_z(box, send, recv, value):
        own = box.at[len(OVER_Z)]
        own[...] = value
        for r, d in enumerate(OVER_Z):
            remote(own, box.at[r], send, recv, d).start()

    def sum_over_z(box, send, recv):
        over_z(box, send, recv).wait_recv()
        return log_sum([box[r] for r in range(len(OVER_Z) + 1)])

    def core_copy(it):
        return remote(core_box.at[it, 1], core_box.at[it, 0], core_send.at[it], core_recv.at[it], OTHER_CORE)

    def core_give(it, value):
        core_box[it, 1] = value
        core_copy(it).start()

    def sum_over_cores(it):
        core_copy(it).wait_recv()
        return log_sum([core_box[it, r] for r in range(2)])

    for i in range(2):
        h = (x & 1) ^ jnp.where(half == c, i, 1 - i)
        here = x == 2 * c + h

        @pl.when(here)
        def _():
            x_in[h] = x_own[...]

        def rows_and_sums(k, _):
            @pl.when(jnp.logical_not(here))
            def _():
                remote(x_in.at[h, k], x_in.at[h, k], x_send, x_recv.at[h, k], OVER_X[0]).wait_recv()

            rows_of(h, k)
            for tile in range(CORES):
                row_sums_at((4 * h + k) * LANES, tile)
            return 0

        lax.fori_loop(0, 4, rows_and_sums, 0)
        row_start(0, h)

    def columns_from_rows(it):
        col_reset()
        for q in range(PARTS):
            f_box[0, q] = row_end(it, q)
            col_sums(q, (0, 1))
        return col_total_of()

    def iteration(it, _):
        mine = columns_from_rows(it)
        give_over_z(col_box.at[it], col_send.at[it], col_recv.at[it], mine)
        core_give(it, sum_over_z(col_box.at[it], col_send.at[it], col_recv.at[it]))
        g = jnp.where(col_live, log_b - sum_over_cores(it), 0.0)
        for b in range(COL_BLOCKS):
            g_rep[b] = jnp.broadcast_to(g[b : b + 1, :], (8, LANES))
        for q in range(PARTS):
            for tile in range(CORES):
                row_sums(q, tile)
            row_start(it + 1, q)
        return 0

    last = ITERS - 1
    lax.fori_loop(0, last, iteration, 0)
    local_sums = columns_from_rows(last)
    core_give(last, local_sums)
    f_copy = remote(f_box.at[0], f_box.at[1], f_sems.at[0], f_sems.at[1], OTHER_CORE)
    f_copy.start()
    for b in range(COL_BLOCKS):
        col_peak[b] = jnp.broadcast_to(local_sums[b : b + 1, :], (8, LANES))

    def distance(k):
        step = (k + 1) // 2
        return jnp.where(lax.rem(k, 2) == 0, 4 + step, 4 - step)

    def give(k):
        return remote(num_give.at[k], num_got.at[k], give_send, give_recv.at[k], OTHER_CORE)

    def ancestors_of(k, _):
        @pl.when(k < Z_CHIPS)
        def _():
            to = lax.rem(z + distance(k), Z_CHIPS)
            cols = [lanes(i * Z_CHIPS + to) for i in range(CORES)]
            local = [col_peak[i * Z_CHIPS + to] for i in range(CORES)]
            acc = jnp.zeros((PAD, CORES * LANES), jnp.float32)
            for r in range(ROWS // 256):
                at = slice(r * 256, (r + 1) * 256)
                f = f_rep[at, :]
                weight = jnp.concatenate(
                    [jnp.exp2(logits[at, cols[i]] + (f - local[i][0:1, :])) for i in range(CORES)], axis=1
                )
                w1, w2 = split(weight, 2)
                two = jnp.dot(x_pieces[:, at], w1, preferred_element_type=jnp.float32)
                acc += two[0:PAD] + two[PAD:] + jnp.dot(x_pieces[0:PAD, at], w2, preferred_element_type=jnp.float32)
            tiles = [acc[0:56, i * LANES : (i + 1) * LANES] for i in range(CORES)]
            num_own[k] = jnp.where(c == 0, tiles[0], tiles[1])
            num_give[k] = jnp.where(c == 0, tiles[1], tiles[0])
            sums = [value[0:1, :] for value in local]
            num_own[k, DIMS : DIMS + 1, :] = jnp.where(c == 0, sums[0], sums[1])
            num_give[k, DIMS : DIMS + 1, :] = jnp.where(c == 0, sums[1], sums[0])
            give(k).start()

        @pl.when(k == 2)
        def _():
            both = sum_over_cores(last)
            give_over_z(g_sum_box, g_sum_sems.at[0], g_sum_sems.at[1], jnp.where(c == 0, both[0:Z_CHIPS], both[Z_CHIPS:]))

        @pl.when(k >= 2)
        def _():
            j = k - 2
            dz = distance(j)
            give(j).wait_recv()
            sums = [box[j, DIMS : DIMS + 1, :] for box in (num_own, num_got)]
            both = log_sum(sums)
            num_send[j] = num_own[j] * jnp.exp2(sums[0] - both) + num_got[j] * jnp.exp2(sums[1] - both)
            num_send[j, DIMS : DIMS + 1, :] = both

            @pl.when(j < Z_CHIPS - 1)
            def _():
                remote(num_send.at[j], num_in.at[j], num_sems.at[0], num_sems.at[1], (dz, 0, 0, 0)).start()

        return 0

    lax.fori_loop(0, Z_CHIPS + 2, ancestors_of, 0)

    live_here = col_within < count_tgt[at_tgt]
    g_here = log_b[0:Z_CHIPS] - sum_over_z(g_sum_box, g_sum_sems.at[0], g_sum_sems.at[1])
    g_here = jnp.where(live_here, g_here * (1.0 / SCALE), 0.0)
    for k in range(Z_CHIPS):
        norm = y_norms[c * Z_CHIPS + k]
        within = (k * X_CHIPS + x) * LANES + lax.broadcasted_iota(jnp.int32, (1, LANES), 1)
        g_box[x, k : k + 1, :] = jnp.where(within < count_tgt[at_tgt], g_here[k : k + 1, :] + norm, 0.0)
    for d in OVER_X:
        remote(g_box.at[x], g_box.at[x], g_sems.at[0], g_sems.at[1], d).start()

    f_copy.wait_recv()
    count_here = count_src[at_src]
    lane = lax.broadcasted_iota(jnp.int32, (1, LANES), 1)
    from_core = jnp.where(half == c, 0, 1)
    for b in range(4):
        at = lax.rem(x, 2) * 4 + b
        f_here = f_box[from_core, at // PART_BLOCKS, lax.rem(at, PART_BLOCKS)]
        value = f_here[None, :] * (1.0 / SCALE) + jnp.sum(x_own[b] * x_own[b], axis=0, keepdims=True)
        f_out[:, b * LANES : (b + 1) * LANES] = jnp.where(b * LANES + lane < count_here, value, 0.0)

    some = num_in.at[pl.ds(0, Z_CHIPS - 1)]
    num_all = remote(some, some, num_sems.at[0], num_sems.at[1], OVER_Z[0])
    num_all.wait_recv()
    parts = [num_in.at[r] for r in range(Z_CHIPS - 1)] + [num_send.at[Z_CHIPS - 1]]
    weigh = [p[DIMS : DIMS + 1, :] for p in parts]
    total = log_sum(weigh)
    acc = jnp.zeros((DIMS, LANES), jnp.float32)
    for p, w in zip(parts, weigh):
        acc += p[0:DIMS, :] * jnp.exp2(w - total)
    anc_out[...] = jnp.where(at_src * LANES + lane < count_tgt[at_tgt], acc, 0.0)

    g_some = remote(g_box.at[pl.ds(0, 3)], g_box.at[pl.ds(0, 3)], g_sems.at[0], g_sems.at[1], OVER_X[0])
    g_some.wait_recv()
    for k in range(Z_CHIPS):
        for i in range(X_CHIPS):
            b = k * X_CHIPS + i
            g_out[:, b * LANES : (b + 1) * LANES] = g_box[i, k : k + 1, :]

    num_all.wait_send()
    g_some.wait_send()
    f_copy.wait_send()
    y_copy.wait_send()
    flag_all.wait_send()
    remote(num_give, num_got, give_send, give_recv.at[0], OTHER_CORE).wait_send()

    @pl.when(half == c)
    def _():
        for copy in x_copies:
            copy.wait_send()

    def sent(it, _):
        for q in range(PARTS):
            row_all(it, q).wait_send()
        return 0

    lax.fori_loop(0, ITERS, sent, 0)
    over_z(g_sum_box, g_sum_sems.at[0], g_sum_sems.at[1]).wait_send()
    for it in range(ITERS):
        core_copy(it).wait_send()
        if it < last:
            over_z(col_box.at[it], col_send.at[it], col_recv.at[it]).wait_send()


def hand_over(f, g, anc, f_out, g_out, anc_out, sems):
    copies = [
        pltpu.make_async_copy(a, b, sems.at[i]) for i, (a, b) in enumerate(((f, f_out), (g, g_out), (anc, anc_out)))
    ]
    for copy in copies:
        copy.start()
    for copy in copies:
        copy.wait()


def in_hbm_now(array):
    return pltpu.with_memory_space_constraint(array, pltpu.HBM)


def shards(sources, targets, pair_active, count_src, count_tgt):
    f32, bf16 = jnp.float32, jnp.bfloat16
    vmem, sem = pltpu.VMEM, pltpu.SemaphoreType.DMA
    in_vmem = pl.BlockSpec(memory_space=pltpu.VMEM)
    in_hbm = pl.BlockSpec(memory_space=pltpu.HBM)
    f, g, anc = pl.pallas_call(
        kernel,
        out_shape=(
            jax.ShapeDtypeStruct((1, 512), f32),
            jax.ShapeDtypeStruct((1, 4096), f32),
            jax.ShapeDtypeStruct((DIMS, LANES), f32),
        ),
        in_specs=[in_hbm] * 5,
        out_specs=(in_vmem, in_vmem, in_vmem),
        scratch_shapes=[
            pltpu.SMEM((32,), jnp.int32),
            pltpu.SMEM((8,), jnp.int32),
            pltpu.SMEM((1, 1), jnp.int32),
            vmem((4, DIMS, LANES), f32),
            vmem((X_CHIPS * CORES, 1, LANES), f32),
            vmem((2, 4, DIMS, LANES), f32),
            vmem((CORES, DIMS, COLS // 2), f32),
            vmem((PAD, ROWS), f32),
            vmem((PAD, COLS), f32),
            vmem((6 * PAD + EXTRA, COLS), bf16),
            vmem((2 * PAD, ROWS), bf16),
            vmem((COL_BLOCKS, 1, LANES), f32),
            vmem((ROWS, COLS), f32),
            vmem((ROWS, LANES), f32),
            vmem((ROWS, LANES), f32),
            vmem((ROWS, LANES), f32),
            vmem((COL_BLOCKS, 8, LANES), f32),
            vmem((COL_BLOCKS, 8, LANES), f32),
            vmem((COL_BLOCKS, 8, LANES), f32),
            vmem((ITERS, PARTS, 16, PART_BLOCKS, LANES), f32),
            vmem((ITERS, Z_CHIPS, COL_BLOCKS, LANES), f32),
            vmem((ITERS, 2, COL_BLOCKS, LANES), f32),
            vmem((Z_CHIPS, Z_CHIPS, LANES), f32),
            vmem((2, PARTS, PART_BLOCKS, LANES), f32),
            vmem((X_CHIPS, Z_CHIPS, LANES), f32),
            vmem((Z_CHIPS, 56, LANES), f32),
            vmem((Z_CHIPS, 56, LANES), f32),
            vmem((Z_CHIPS, 56, LANES), f32),
            vmem((Z_CHIPS, 56, LANES), f32),
            vmem((Z_CHIPS, 56, LANES), f32),
            sem((7 + Z_CHIPS,)), sem((2,)), sem(()), sem((2, 4)), sem((2,)), sem((ITERS, PARTS)), sem((ITERS, PARTS)),
            sem((ITERS,)), sem((ITERS,)), sem((ITERS,)), sem((ITERS,)), sem((2,)), sem((2,)), sem((2,)),
            sem(()), sem((Z_CHIPS,)), sem((2,)),
        ],
        compiler_params=pltpu.CompilerParams(
            collective_id=0, has_side_effects=True, vmem_limit_bytes=40 * 2**20
        ),
    )(in_hbm_now(count_src), in_hbm_now(count_tgt), pair_active, in_hbm_now(sources), in_hbm_now(targets))
    f, g, anc = pl.pallas_call(
        hand_over,
        out_shape=(
            jax.ShapeDtypeStruct((1, 512), f32),
            jax.ShapeDtypeStruct((1, 4096), f32),
            jax.ShapeDtypeStruct((DIMS, LANES), f32),
        ),
        in_specs=[pl.BlockSpec(memory_space=pl.ANY)] * 3,
        out_specs=(in_hbm,) * 3,
        scratch_shapes=[sem((3,))],
        compiler_params=pltpu.CompilerParams(vmem_limit_bytes=40 * 2**20),
    )(f, g, anc)
    return f.reshape(512), g.reshape(4096), anc


def solution(mesh):
    return jax.shard_map(
        shards,
        mesh=mesh,
        in_specs=(P(None, "src"), P(None, "tgt"), P("src", "tgt"), P(), P()),
        out_specs=(P("src"), P("tgt"), P(None, ("tgt", "src"))),
        check_vma=False,
    )
```

```python
import math

import jax
import jax.numpy as jnp
from jax import lax
from jax.experimental import pallas as pl
from jax.experimental.pallas import tpu as pltpu
from jax.sharding import PartitionSpec as P

ITERS = 4
EPS = 0.02
SCALE = math.log2(math.e) / EPS
NEG = -(2.0**100)
LOW = -3.0e38
LOGICAL = pl.DeviceIdType.LOGICAL

DIMS = 50
PAD = 64
EXTRA = 16
ROWS = 1024
COLS = 2048
LANES = 128
COL_BLOCKS = COLS // LANES
PARTS = 2
PART_BLOCKS = ROWS // LANES // PARTS
PART_ROWS = ROWS // PARTS
X_CHIPS = 4
Y_CHIPS = 4
Z_CHIPS = 8
CORES = 2

OVER_XY = sorted(
    [(0, dx, dy, 0) for dx in range(X_CHIPS) for dy in range(Y_CHIPS) if dx or dy],
    key=lambda d: -(min(d[1], X_CHIPS - d[1]) + min(d[2], Y_CHIPS - d[2])),
)
OVER_Z = sorted([(dz, 0, 0, 0) for dz in range(1, Z_CHIPS)], key=lambda d: -min(d[0], Z_CHIPS - d[0]))
OVER_X_CORE = [(0, dx, 0, dc) for dx in range(X_CHIPS) for dc in range(CORES) if dx or dc]
OVER_X = [(0, 2, 0, 0), (0, 1, 0, 0), (0, 3, 0, 0)]
OTHER_CORE = (0, 0, 0, 1)
PARTNERS = OVER_XY + OVER_Z + [OTHER_CORE] + [d for d in OVER_X_CORE if d[1] and d[3]]


def tree(op, parts):
    while len(parts) > 1:
        parts = [op(*parts[i : i + 2]) if i + 1 < len(parts) else parts[i] for i in range(0, len(parts), 2)]
    return parts[0]


def log_sum(parts):
    peak = tree(jnp.maximum, parts)
    total = tree(jnp.add, [jnp.exp2(p - peak) for p in parts])
    return peak + jnp.log2(total)


def split(value, pieces):
    out = []
    for _ in range(pieces):
        piece = value.astype(jnp.bfloat16)
        out.append(piece)
        value = value - piece.astype(jnp.float32)
    return out


def kernel(
    counts_src, counts_tgt, pairs, src, tgt,
    f_out, g_out, anc_out,
    count_src, count_tgt, pair, x_own, flags, x_in, y_in, x_full, y_full, y_stack, x_pieces, y_norms,
    logits, row_peak, row_total, f_rep, g_rep, col_peak, col_total,
    row_box, col_box, core_box, g_sum_box, f_box, g_box, num_own, num_give, num_got, num_send, num_in,
    own_sems, flag_sems, x_send, x_recv, y_sems, row_send, row_recv, col_send, col_recv, core_send, core_recv, g_sum_sems, f_sems, g_sems,
    give_send, give_recv, num_sems,
):
    at_src = lax.axis_index("src")
    at_tgt = lax.axis_index("tgt")
    z, x = at_src // X_CHIPS, at_src & (X_CHIPS - 1)
    y, c = at_tgt // CORES, at_tgt & (CORES - 1)
    half = x // 2

    def device(d):
        dz, dx, dy, dc = d
        at_z = (z + dz) & (Z_CHIPS - 1) if not isinstance(dz, int) or dz else z
        at_x = (x + dx) & (X_CHIPS - 1) if dx else x
        at_y = (y + dy) & (Y_CHIPS - 1) if dy else y
        at_c = c ^ dc
        return ((at_z * X_CHIPS + at_x) * Y_CHIPS + at_y) * CORES + at_c

    ids = {d: device(d) for d in PARTNERS}

    def remote(a, b, send, recv, d):
        return pltpu.make_async_remote_copy(
            src_ref=a, dst_ref=b, send_sem=send, recv_sem=recv, device_id=ids[d] if isinstance(d[0], int) else device(d), device_id_type=LOGICAL
        )

    def lanes(k, width=LANES):
        return pl.ds(pl.multiple_of(k * width, width), width)

    barrier = pltpu.get_barrier_semaphore()
    for d in PARTNERS:
        pl.semaphore_signal(barrier, inc=1, device_id=ids[d], device_id_type=LOGICAL)

    x_local = [pltpu.make_async_copy(src.at[:, lanes(k)], x_own.at[k], own_sems.at[k]) for k in range(4)]
    for copy in x_local:
        copy.start()
    y_local = [
        pltpu.make_async_copy(tgt.at[:, lanes(k * X_CHIPS + x)], y_in.at[c, :, lanes(k)], own_sems.at[4 + k])
        for k in range(Z_CHIPS)
    ]
    for copy in y_local:
        copy.start()
    scalars = [
        pltpu.make_async_copy(a, b, own_sems.at[4 + Z_CHIPS + i])
        for i, (a, b) in enumerate(((counts_src, count_src), (counts_tgt, count_tgt), (pairs, pair)))
    ]
    for copy in scalars:
        copy.start()
    pl.semaphore_wait(barrier, len(PARTNERS))

    x_copies = [
        remote(src.at[:, lanes(k)], x_in.at[x & 1, k], x_send, x_recv.at[x & 1, k], d) for k in range(4) for d in OVER_X
    ]

    @pl.when(half == c)
    def _():
        for copy in x_copies:
            copy.start()

    for k in range(Z_CHIPS):
        whole = tgt.at[:, lanes(k * X_CHIPS + x)]
        remote(whole, y_in.at[c, :, lanes(k)], y_sems.at[0], y_sems.at[1], OTHER_CORE).start()
    y_copy = remote(y_in.at[1 - c], y_in.at[1 - c], y_sems.at[0], y_sems.at[1], OTHER_CORE)

    for copy in scalars:
        copy.wait()
    mine = x * CORES + c
    listed = (pair[0, 0] > 0).astype(jnp.float32)
    flags[mine] = jnp.full((1, LANES), listed, jnp.float32)
    for d in OVER_X_CORE:
        remote(flags.at[mine], flags.at[mine], flag_sems.at[0], flag_sems.at[1], d).start()

    def number_of(counts, length):
        total = counts[0]
        for i in range(1, length):
            total = total + counts[i]
        return total.astype(jnp.float32)

    log_a = -jnp.log2(jnp.full((PART_BLOCKS, LANES), number_of(count_src, Z_CHIPS * X_CHIPS), jnp.float32))
    log_b = -jnp.log2(jnp.full((COL_BLOCKS, LANES), number_of(count_tgt, Y_CHIPS * CORES), jnp.float32))
    col_counts = [count_tgt[y * CORES + i] for i in range(CORES)]

    def places(shape):
        return lax.broadcasted_iota(jnp.int32, shape, 0), lax.broadcasted_iota(jnp.int32, shape, 1)

    def row_live(q):
        block, lane = places((PART_BLOCKS, LANES))
        within = (lax.rem(q * PART_BLOCKS, 4) + block) * LANES + lane
        return within < count_src[z * X_CHIPS + 2 * c + q * PART_BLOCKS // 4]

    block, lane = places((Z_CHIPS, LANES))
    col_within = (block * X_CHIPS + x) * LANES + lane
    two_within = jnp.concatenate([col_within] * CORES, axis=0)
    two_block = lax.broadcasted_iota(jnp.int32, (COL_BLOCKS, LANES), 0)
    col_live = two_within < jnp.where(two_block < Z_CHIPS, col_counts[0], col_counts[1])

    x_full[DIMS:PAD, :] = jnp.zeros((PAD - DIMS, ROWS), jnp.float32)
    y_full[DIMS:PAD, :] = jnp.zeros((PAD - DIMS, COLS), jnp.float32)

    def columns_of(tile):
        y_full[0:DIMS, lanes(tile, COLS // 2)] = y_in[tile]

        def body(k, _):
            b = tile * Z_CHIPS + k
            whole = y_full[:, lanes(b)]
            norm = jnp.sum(whole * whole, axis=0, keepdims=True)
            y_norms[b] = norm
            g_rep[b] = jnp.broadcast_to(-SCALE * norm, (8, LANES))
            p1, p2, p3 = split(whole, 3)
            for i, p in enumerate((p1, p2, p1, p3, p1, p2)):
                y_stack[i * PAD : (i + 1) * PAD, lanes(b)] = p
            return 0

        lax.fori_loop(0, Z_CHIPS, body, 0)

    for copy in x_local + y_local:
        copy.wait()
    columns_of(c)
    y_copy.wait_recv()
    columns_of(1 - c)
    flag_some = flags.at[pl.ds(0, len(OVER_X_CORE))]
    flag_all = remote(flag_some, flag_some, flag_sems.at[0], flag_sems.at[1], OTHER_CORE)
    flag_all.wait_recv()
    line, lane = places((EXTRA, LANES))
    for b in range(COL_BLOCKS):
        tile, k = b // Z_CHIPS, b % Z_CHIPS
        dead = jnp.where((k * X_CHIPS + x) * LANES + lane < col_counts[tile], 0.0, NEG)
        rows = [jnp.minimum(jnp.where(flags[(2 * c + i) * CORES + tile] > 0, 0.0, NEG), dead) for i in range(2)]
        extra = jnp.where(line == 0, rows[0], jnp.where(line == 1, rows[1], jnp.where(line == 2, 1.0, 0.0)))
        y_stack[6 * PAD :, b * LANES : (b + 1) * LANES] = extra.astype(jnp.bfloat16)

    def rows_of(h, pair):
        live = count_src[z * X_CHIPS + 2 * c + h]
        lines = []
        for i in range(2):
            k = 2 * pair + i
            at = lanes(4 * h + k)
            x_full[0:DIMS, at] = x_in[h, k]
            p1, p2, p3 = split(x_full[:, at] * (2.0 * SCALE), 3)
            dead = jnp.where(k * LANES + lane < live, 0.0, NEG)
            extra = jnp.where(line == 2, dead, jnp.where(line == h, 1.0, 0.0))
            lines.append(jnp.concatenate([p1, p1, p2, p1, p3, p2, extra.astype(jnp.bfloat16)], axis=0).T)
        rows = jnp.concatenate(lines, axis=0)
        at = lanes(2 * h + pair, 2 * LANES)
        here, peaks, totals = logits.at[at], row_peak.at[at], row_total.at[at]
        for i in range(COLS // 256):
            cols = slice(i * 256, (i + 1) * 256)
            here[:, cols] = jnp.dot(rows, y_stack[:, cols], preferred_element_type=jnp.float32)
            if i == 3:
                row_sums_in(here, peaks, totals, 0)
        row_sums_in(here, peaks, totals, 1)

    def pieces_of(k, _):
        first, second = split(x_full[:, lanes(k)], 2)
        x_pieces[0:PAD, lanes(k)] = first
        x_pieces[PAD:, lanes(k)] = second
        return 0

    def row_all(it, q):
        some = row_box.at[it, q, pl.ds(0, len(OVER_XY))]
        return remote(some, some, row_send.at[it, q], row_recv.at[it, q], OVER_XY[0])

    def row_sums_in(here, peaks, totals, tile):
        g = [g_rep[tile * 8 + b] for b in range(8)]
        for i in range(here.shape[0] // 8):
            at = slice(8 * i, 8 * i + 8)
            parts = [here[at, (tile * 8 + b) * LANES : (tile * 8 + b + 1) * LANES] + g[b] for b in range(8)]
            best = tree(jnp.maximum, parts)
            if tile:
                peak = peaks[at, :]
                best = jnp.maximum(best, peak)
            total = tree(jnp.add, [jnp.exp2(p - best) for p in parts])
            if tile:
                total += totals[at, :] * jnp.exp2(peak - best)
            peaks[at, :] = best
            totals[at, :] = total

    def row_sums(q):
        def body(k, _):
            at = lanes(q * PART_BLOCKS + k)
            for tile in range(CORES):
                row_sums_in(logits.at[at], row_peak.at[at], row_total.at[at], tile)
            return 0

        lax.fori_loop(0, PART_BLOCKS, body, 0, unroll=2)

    def row_start(it, q):
        own = row_box.at[it, q, len(OVER_XY)]
        for b in range(PART_BLOCKS):
            peaks = row_peak[lanes(PART_BLOCKS * q + b), :].T
            totals = row_total[lanes(PART_BLOCKS * q + b), :].T
            peak = jnp.max(peaks, axis=0, keepdims=True)
            total = jnp.sum(totals * jnp.exp2(peaks - peak), axis=0, keepdims=True)
            own[b : b + 1, :] = peak + jnp.log2(total)
        for r, d in enumerate(OVER_XY):
            remote(own, row_box.at[it, q, r], row_send.at[it, q], row_recv.at[it, q], d).start()

    def row_end(it, q):
        row_all(it, q).wait_recv()
        total = log_sum([row_box[it, q, r] for r in range(len(OVER_XY) + 1)])
        f = jnp.where(row_live(q), log_a - total, 0.0)
        for b in range(PART_BLOCKS):
            f_rep[lanes(PART_BLOCKS * q + b), :] = jnp.broadcast_to(f[b : b + 1, :], (LANES, LANES)).T
        return f

    def col_sums(q, tiles):
        def body(k, _):
            base = q * PART_ROWS + k * 64
            f = [f_rep[pl.ds(pl.multiple_of(base + 8 * j, 8), 8), :] for j in range(8)]
            for tile in tiles:
                for b in range(tile * 8, tile * 8 + 8):
                    parts = [
                        logits[pl.ds(pl.multiple_of(base + 8 * j, 8), 8), b * LANES : (b + 1) * LANES] + f[j]
                        for j in range(8)
                    ]
                    peak = col_peak[b]
                    best = jnp.maximum(peak, tree(jnp.maximum, parts))
                    fresh = tree(jnp.add, [jnp.exp2(p - best) for p in parts])
                    col_total[b] = col_total[b] * jnp.exp2(peak - best) + fresh
                    col_peak[b] = best
            return 0

        lax.fori_loop(0, PART_ROWS // 64, body, 0, unroll=4)

    def col_reset():
        col_peak[...] = jnp.full((COL_BLOCKS, 8, LANES), LOW, jnp.float32)
        col_total[...] = jnp.zeros((COL_BLOCKS, 8, LANES), jnp.float32)

    def col_total_of():
        peaks = col_peak[...]
        peak = jnp.max(peaks, axis=1, keepdims=True)
        total = jnp.sum(col_total[...] * jnp.exp2(peaks - peak), axis=1)
        return peak[:, 0, :] + jnp.log2(total)

    def over_z(box, send, recv):
        some = box.at[pl.ds(0, len(OVER_Z))]
        return remote(some, some, send, recv, OVER_Z[0])

    def give_over_z(box, send, recv, value):
        own = box.at[len(OVER_Z)]
        own[...] = value
        for r, d in enumerate(OVER_Z):
            remote(own, box.at[r], send, recv, d).start()

    def sum_over_z(box, send, recv):
        over_z(box, send, recv).wait_recv()
        return log_sum([box[r] for r in range(len(OVER_Z) + 1)])

    def core_copy(it):
        return remote(core_box.at[it, 1], core_box.at[it, 0], core_send.at[it], core_recv.at[it], OTHER_CORE)

    def core_give(it, value):
        core_box[it, 1] = value
        core_copy(it).start()

    def sum_over_cores(it):
        core_copy(it).wait_recv()
        return log_sum([core_box[it, r] for r in range(2)])

    for i in range(2):
        h = (x & 1) ^ jnp.where(half == c, i, 1 - i)
        here = x == 2 * c + h

        @pl.when(here)
        def _():
            x_in[h] = x_own[...]

        def rows_and_sums(pair, _):
            @pl.when(jnp.logical_not(here))
            def _():
                for i in range(2):
                    k = 2 * pair + i
                    remote(x_in.at[h, k], x_in.at[h, k], x_send, x_recv.at[h, k], OVER_X[0]).wait_recv()

            rows_of(h, pair)
            return 0

        lax.fori_loop(0, 2, rows_and_sums, 0)
        row_start(0, h)

    lax.fori_loop(0, 2 * 4, pieces_of, 0)

    def columns_from_rows(it):
        col_reset()
        for q in range(PARTS):
            f_box[0, q] = row_end(it, q)
            col_sums(q, (0, 1))
        return col_total_of()

    def iteration(it, _):
        mine = columns_from_rows(it)
        give_over_z(col_box.at[it], col_send.at[it], col_recv.at[it], mine)
        core_give(it, sum_over_z(col_box.at[it], col_send.at[it], col_recv.at[it]))
        g = jnp.where(col_live, log_b - sum_over_cores(it), 0.0)
        for b in range(COL_BLOCKS):
            g_rep[b] = jnp.broadcast_to(g[b : b + 1, :], (8, LANES))
        for q in range(PARTS):
            row_sums(q)
            row_start(it + 1, q)
        return 0

    last = ITERS - 1
    lax.fori_loop(0, last, iteration, 0)
    local_sums = columns_from_rows(last)
    core_give(last, local_sums)
    f_copy = remote(f_box.at[0], f_box.at[1], f_sems.at[0], f_sems.at[1], OTHER_CORE)
    f_copy.start()
    for b in range(COL_BLOCKS):
        col_peak[b] = jnp.broadcast_to(local_sums[b : b + 1, :], (8, LANES))

    def distance(k):
        step = (k + 1) // 2
        return jnp.where(lax.rem(k, 2) == 0, 4 + step, 4 - step)

    def give(k):
        return remote(num_give.at[k], num_got.at[k], give_send, give_recv.at[k], OTHER_CORE)

    def ancestors_of(k, _):
        @pl.when(k < Z_CHIPS)
        def _():
            to = lax.rem(z + distance(k), Z_CHIPS)
            cols = [lanes(i * Z_CHIPS + to) for i in range(CORES)]
            local = [col_peak[i * Z_CHIPS + to] for i in range(CORES)]
            acc = jnp.zeros((PAD, CORES * LANES), jnp.float32)
            for r in range(ROWS // 256):
                at = slice(r * 256, (r + 1) * 256)
                f = f_rep[at, :]
                weight = jnp.concatenate(
                    [jnp.exp2(logits[at, cols[i]] + (f - local[i][0:1, :])) for i in range(CORES)], axis=1
                )
                w1, w2 = split(weight, 2)
                two = jnp.dot(x_pieces[:, at], w1, preferred_element_type=jnp.float32)
                acc += two[0:PAD] + two[PAD:] + jnp.dot(x_pieces[0:PAD, at], w2, preferred_element_type=jnp.float32)
            tiles = [acc[0 : DIMS + 1, i * LANES : (i + 1) * LANES] for i in range(CORES)]
            num_own[k] = jnp.where(c == 0, tiles[0], tiles[1])
            num_give[k] = jnp.where(c == 0, tiles[1], tiles[0])
            sums = [value[0:1, :] for value in local]
            num_own[k, DIMS : DIMS + 1, :] = jnp.where(c == 0, sums[0], sums[1])
            num_give[k, DIMS : DIMS + 1, :] = jnp.where(c == 0, sums[1], sums[0])
            give(k).start()

        @pl.when(k == 2)
        def _():
            both = sum_over_cores(last)
            give_over_z(g_sum_box, g_sum_sems.at[0], g_sum_sems.at[1], jnp.where(c == 0, both[0:Z_CHIPS], both[Z_CHIPS:]))

        @pl.when(k >= 2)
        def _():
            j = k - 2
            dz = distance(j)
            give(j).wait_recv()
            sums = [box[j, DIMS : DIMS + 1, :] for box in (num_own, num_got)]
            both = log_sum(sums)
            num_send[j] = num_own[j] * jnp.exp2(sums[0] - both) + num_got[j] * jnp.exp2(sums[1] - both)
            num_send[j, DIMS : DIMS + 1, :] = both

            @pl.when(j < Z_CHIPS - 1)
            def _():
                remote(num_send.at[j], num_in.at[j], num_sems.at[0], num_sems.at[1], (dz, 0, 0, 0)).start()

        return 0

    lax.fori_loop(0, Z_CHIPS + 2, ancestors_of, 0)

    live_here = col_within < count_tgt[at_tgt]
    g_here = log_b[0:Z_CHIPS] - sum_over_z(g_sum_box, g_sum_sems.at[0], g_sum_sems.at[1])
    g_here = jnp.where(live_here, g_here * (1.0 / SCALE), 0.0)
    for k in range(Z_CHIPS):
        norm = y_norms[c * Z_CHIPS + k]
        within = (k * X_CHIPS + x) * LANES + lax.broadcasted_iota(jnp.int32, (1, LANES), 1)
        g_box[x, k : k + 1, :] = jnp.where(within < count_tgt[at_tgt], g_here[k : k + 1, :] + norm, 0.0)
    for d in OVER_X:
        remote(g_box.at[x], g_box.at[x], g_sems.at[0], g_sems.at[1], d).start()

    f_copy.wait_recv()
    count_here = count_src[at_src]
    lane = lax.broadcasted_iota(jnp.int32, (1, LANES), 1)
    from_core = jnp.where(half == c, 0, 1)
    for b in range(4):
        at = lax.rem(x, 2) * 4 + b
        f_here = f_box[from_core, at // PART_BLOCKS, lax.rem(at, PART_BLOCKS)]
        value = f_here[None, :] * (1.0 / SCALE) + jnp.sum(x_own[b] * x_own[b], axis=0, keepdims=True)
        f_out[:, b * LANES : (b + 1) * LANES] = jnp.where(b * LANES + lane < count_here, value, 0.0)

    some = num_in.at[pl.ds(0, Z_CHIPS - 1)]
    num_all = remote(some, some, num_sems.at[0], num_sems.at[1], OVER_Z[0])
    num_all.wait_recv()
    parts = [num_in.at[r] for r in range(Z_CHIPS - 1)] + [num_send.at[Z_CHIPS - 1]]
    weigh = [p[DIMS : DIMS + 1, :] for p in parts]
    total = log_sum(weigh)
    acc = jnp.zeros((DIMS, LANES), jnp.float32)
    for p, w in zip(parts, weigh):
        acc += p[0:DIMS, :] * jnp.exp2(w - total)
    anc_out[...] = jnp.where(at_src * LANES + lane < count_tgt[at_tgt], acc, 0.0)

    g_some = remote(g_box.at[pl.ds(0, 3)], g_box.at[pl.ds(0, 3)], g_sems.at[0], g_sems.at[1], OVER_X[0])
    g_some.wait_recv()
    for k in range(Z_CHIPS):
        for i in range(X_CHIPS):
            b = k * X_CHIPS + i
            g_out[:, b * LANES : (b + 1) * LANES] = g_box[i, k : k + 1, :]

    num_all.wait_send()
    g_some.wait_send()
    f_copy.wait_send()
    y_copy.wait_send()
    flag_all.wait_send()
    remote(num_give, num_got, give_send, give_recv.at[0], OTHER_CORE).wait_send()

    @pl.when(half == c)
    def _():
        for copy in x_copies:
            copy.wait_send()

    def sent(it, _):
        for q in range(PARTS):
            row_all(it, q).wait_send()
        return 0

    lax.fori_loop(0, ITERS, sent, 0)
    over_z(g_sum_box, g_sum_sems.at[0], g_sum_sems.at[1]).wait_send()
    for it in range(ITERS):
        core_copy(it).wait_send()
        if it < last:
            over_z(col_box.at[it], col_send.at[it], col_recv.at[it]).wait_send()


def hand_over(f, g, anc, f_out, g_out, anc_out, sems):
    copies = [
        pltpu.make_async_copy(a, b, sems.at[i]) for i, (a, b) in enumerate(((f, f_out), (g, g_out), (anc, anc_out)))
    ]
    for copy in copies:
        copy.start()
    for copy in copies:
        copy.wait()


def in_hbm_now(array):
    return pltpu.with_memory_space_constraint(array, pltpu.HBM)


def shards(sources, targets, pair_active, count_src, count_tgt):
    f32, bf16 = jnp.float32, jnp.bfloat16
    vmem, sem = pltpu.VMEM, pltpu.SemaphoreType.DMA
    in_vmem = pl.BlockSpec(memory_space=pltpu.VMEM)
    in_hbm = pl.BlockSpec(memory_space=pltpu.HBM)
    f, g, anc = pl.pallas_call(
        kernel,
        out_shape=(
            jax.ShapeDtypeStruct((1, 512), f32),
            jax.ShapeDtypeStruct((1, 4096), f32),
            jax.ShapeDtypeStruct((DIMS, LANES), f32),
        ),
        in_specs=[in_hbm] * 5,
        out_specs=(in_vmem, in_vmem, in_vmem),
        scratch_shapes=[
            pltpu.SMEM((32,), jnp.int32),
            pltpu.SMEM((8,), jnp.int32),
            pltpu.SMEM((1, 1), jnp.int32),
            vmem((4, DIMS, LANES), f32),
            vmem((X_CHIPS * CORES, 1, LANES), f32),
            vmem((2, 4, DIMS, LANES), f32),
            vmem((CORES, DIMS, COLS // 2), f32),
            vmem((PAD, ROWS), f32),
            vmem((PAD, COLS), f32),
            vmem((6 * PAD + EXTRA, COLS), bf16),
            vmem((2 * PAD, ROWS), bf16),
            vmem((COL_BLOCKS, 1, LANES), f32),
            vmem((ROWS, COLS), f32),
            vmem((ROWS, LANES), f32),
            vmem((ROWS, LANES), f32),
            vmem((ROWS, LANES), f32),
            vmem((COL_BLOCKS, 8, LANES), f32),
            vmem((COL_BLOCKS, 8, LANES), f32),
            vmem((COL_BLOCKS, 8, LANES), f32),
            vmem((ITERS, PARTS, 16, PART_BLOCKS, LANES), f32),
            vmem((ITERS, Z_CHIPS, COL_BLOCKS, LANES), f32),
            vmem((ITERS, 2, COL_BLOCKS, LANES), f32),
            vmem((Z_CHIPS, Z_CHIPS, LANES), f32),
            vmem((2, PARTS, PART_BLOCKS, LANES), f32),
            vmem((X_CHIPS, Z_CHIPS, LANES), f32),
            vmem((Z_CHIPS, DIMS + 1, LANES), f32),
            vmem((Z_CHIPS, DIMS + 1, LANES), f32),
            vmem((Z_CHIPS, DIMS + 1, LANES), f32),
            vmem((Z_CHIPS, DIMS + 1, LANES), f32),
            vmem((Z_CHIPS, DIMS + 1, LANES), f32),
            sem((7 + Z_CHIPS,)), sem((2,)), sem(()), sem((2, 4)), sem((2,)), sem((ITERS, PARTS)), sem((ITERS, PARTS)),
            sem((ITERS,)), sem((ITERS,)), sem((ITERS,)), sem((ITERS,)), sem((2,)), sem((2,)), sem((2,)),
            sem(()), sem((Z_CHIPS,)), sem((2,)),
        ],
        compiler_params=pltpu.CompilerParams(
            collective_id=0, has_side_effects=True, vmem_limit_bytes=40 * 2**20
        ),
    )(in_hbm_now(count_src), in_hbm_now(count_tgt), pair_active, in_hbm_now(sources), in_hbm_now(targets))
    f, g, anc = pl.pallas_call(
        hand_over,
        out_shape=(
            jax.ShapeDtypeStruct((1, 512), f32),
            jax.ShapeDtypeStruct((1, 4096), f32),
            jax.ShapeDtypeStruct((DIMS, LANES), f32),
        ),
        in_specs=[pl.BlockSpec(memory_space=pl.ANY)] * 3,
        out_specs=(in_hbm,) * 3,
        scratch_shapes=[sem((3,))],
        compiler_params=pltpu.CompilerParams(vmem_limit_bytes=40 * 2**20),
    )(f, g, anc)
    return f.reshape(512), g.reshape(4096), anc


def solution(mesh):
    return jax.shard_map(
        shards,
        mesh=mesh,
        in_specs=(P(None, "src"), P(None, "tgt"), P("src", "tgt"), P(), P()),
        out_specs=(P("src"), P("tgt"), P(None, ("tgt", "src"))),
        check_vma=False,
    )
```
